256 devices in a mesh: rows: 32 (over y, x, core), cols: 8 (over z).
Axes of the slice: x: 4, y: 4, z: 8, core: 2. Of those that a mesh axis runs over, the one named last changes fastest.
Arguments:
- eigvecs: float32 [65536, 4096], P('rows', 'cols'), may hold values from -6 to 6
- reflectors: float32 [4, 65536, 256], P(None, 'rows', 'cols'), may hold values from -0.0234375 to 0.0234375
- t_factors: float32 [4, 256, 256], replicated, may hold values from -1 to 3, as said below
Outputs:
- transformed: float32 [65536, 4096], P('rows', 'cols')
The draws below stay inside these ranges and needn't reach their ends.
Inputs may be any that keep to these rules, and one draw needn't show every extreme that they name: Each t_factors[p] is upper triangular with a diagonal between 1 and 3.
All inputs are finite; a program needn't handle non-finite values.
Results may differ from the reference program's by a relative error of at most 0.00011.
Values sent between devices are 32-bit elements; how exact they have to be, the bound alone decides.
A program may use at most 64 MiB of HBM per device.

```python
import jax
import jax.numpy as jnp
from jax import lax

BLOCK = 256
PANELS = 4
N = 65536
K = 4096


def draw_t_factors(key, part):
    key = jax.random.fold_in(key, 5)
    key_diag, key_off = jax.random.split(key)
    diag = jax.random.uniform(key_diag, (PANELS, BLOCK), jnp.float32, 1.5, 2.5)
    off = jax.random.normal(key_off, (PANELS, BLOCK, BLOCK), jnp.float32) / jnp.sqrt(jnp.float32(BLOCK))
    off = jnp.clip(off, -0.9, 0.9)
    row_ids = lax.broadcasted_iota(jnp.int32, (BLOCK, BLOCK), 0)
    col_ids = lax.broadcasted_iota(jnp.int32, (BLOCK, BLOCK), 1)
    upper = jnp.where(row_ids < col_ids, off, jnp.float32(0.0))
    ident = jnp.where(row_ids == col_ids, jnp.float32(1.0), jnp.float32(0.0))
    return upper + diag[:, :, None] * ident[None, :, :]


def levels(own_key, shape, pieces, least, top_value):
    loudness, own = 1.0, jax.random.fold_in(own_key, 6)
    for axis_at, parts in pieces:
        steps = jnp.exp(jax.random.uniform(jax.random.fold_in(own, axis_at), (parts,), jnp.float32, least / len(pieces), top_value / len(pieces)))
        loudness = loudness * jnp.repeat(steps, shape[axis_at] // parts).reshape([-1 if axis == axis_at else 1 for axis in range(len(shape))])
    return loudness


def centred(rng, dims, deviation, limit, shards=(), dtype=jnp.bfloat16):
    level = levels(rng, dims, shards, -0.22, 0.18) if shards else 1.0
    drawn = jax.random.normal(rng, dims, jnp.float32) * deviation * level
    return jnp.minimum(jnp.maximum(drawn, -limit), limit).astype(dtype)


def setup_inputs(seed: int = 0) -> dict:
    seeds = jax.random.split(jax.random.key(seed), 4)
    eigvecs = centred(seeds[0], (N, K), 1.0, 6.0, ((0, 32), (1, 8)), jnp.float32)
    reflectors = centred(seeds[1], (PANELS, N, BLOCK), N ** -0.5, 0.0234375, ((1, 32), (2, 8)), jnp.float32)
    t_factors = draw_t_factors(jax.random.fold_in(seeds[3], 71), 0)
    return dict(eigvecs=eigvecs, reflectors=reflectors, t_factors=t_factors)


def reference(eigvecs, reflectors, t_factors):
    hi = lax.Precision.HIGHEST
    field = eigvecs
    for index in range(PANELS):
        panel = reflectors[index]
        inner = lax.dot_general(panel, field, (((0,), (0,)), ((), ())), precision=hi, preferred_element_type=jnp.float32)
        coeffs = jnp.dot(t_factors[index], inner, precision=hi, preferred_element_type=jnp.float32)
        field = field - jnp.dot(panel, coeffs, precision=hi, preferred_element_type=jnp.float32)
    return field
```

```python
import functools

import jax
import jax.numpy as jnp
from jax import lax
from jax.experimental import pallas as pl
from jax.experimental.pallas import tpu as pltpu
from jax.sharding import PartitionSpec as P

MESH = pl.DeviceIdType.MESH
F32, BF16 = jnp.float32, jnp.bfloat16
PIECE = 8
TILE = 256


def halves(value):
    high = value.astype(BF16)
    return high, (value - high.astype(F32)).astype(BF16)


def product(left, right):
    (left_high, left_low), (right_high, right_low) = left, right
    dot = functools.partial(jnp.dot, preferred_element_type=F32)
    return dot(left_high, right_high) + (dot(left_high, right_low) + dot(left_low, right_high))


def kernel(
    field_in, refl_in, factor_in, out_ref,
    panel, field, high, low, plain_high, plain_low, factors, coef_high, coef_low,
    part, pair, half, spread, sums,
    z_send, z_recv, rs_send, rs_recv, ag_send, ag_recv, core_send, core_recv, own_sem, in_sem, out_sem,
):
    row, z = lax.axis_index("rows"), lax.axis_index("cols")
    core, chip = row % 2, row // 2
    x, y = chip % 4, chip // 4
    z_next = ((row, (z + 1) % 8), (row, (z + 7) % 8))
    twin = (chip * 2 + 1 - core, z)

    def chip_at(k):
        return ((y + k // 4) % 4) * 4 + (x + k % 4) % 4

    def chip_device(k):
        return (chip_at(k) * 2 + core, z)

    panels, blocks = panel.shape[0], field.shape[0] // TILE

    load_field = pltpu.make_async_copy(field_in, field, in_sem.at[0])
    load_factors = pltpu.make_async_copy(factor_in, factors, in_sem.at[1])
    load_field.start()
    load_factors.start()

    def own(p, c):
        return pltpu.make_async_copy(refl_in.at[p, pl.ds(PIECE * c, PIECE)], panel.at[p, z * 4 + c], own_sem.at[p, c])

    for p in range(panels):
        for c in range(4):
            own(p, c).start()

    barrier = pltpu.get_barrier_semaphore()
    for device in (*z_next, twin):
        pl.semaphore_signal(barrier, inc=1, device_id=device, device_id_type=MESH)

    def greet(k, carry):
        pl.semaphore_signal(barrier, inc=1, device_id=chip_device(k), device_id_type=MESH)
        return carry

    lax.fori_loop(1, 16, greet, 0)
    load_field.wait()

    def split(i, carry):
        rows = pl.ds(pl.multiple_of(i * TILE, TILE), TILE)
        high[rows, :], low[rows, :] = halves(field[rows, :])
        return carry

    lax.fori_loop(0, blocks, split, 0)
    pl.semaphore_wait(barrier, 18)

    def hop(p, way, s, c):
        c = c if way == 0 else 3 - c
        owner = (z + 8 - s) % 8 if way == 0 else (z + s) % 8
        source = refl_in.at[p, pl.ds(PIECE * c, PIECE)] if s == 0 else panel.at[p, owner * 4 + c]
        return pltpu.make_async_remote_copy(
            src_ref=source, dst_ref=panel.at[p, owner * 4 + c],
            send_sem=z_send.at[p, way, s, c], recv_sem=z_recv.at[p, way, s, c],
            device_id=z_next[way], device_id_type=MESH,
        )

    def landed(p, way, s, c):
        c = c if way == 0 else 3 - c
        owner = (z + 7 - s) % 8 if way == 0 else (z + 1 + s) % 8
        place = panel.at[p, owner * 4 + c]
        pltpu.make_async_remote_copy(
            src_ref=place, dst_ref=place,
            send_sem=z_send.at[p, way, s, c], recv_sem=z_recv.at[p, way, s, c],
            device_id=z_next[way], device_id_type=MESH,
        ).wait_recv()

    def slots(p, first, last):
        for i in range(first, last):
            s, c = i // 4, i % 4
            for way in (0, 1):
                if s:
                    landed(p, way, s - 1, c)
                hop(p, way, s, c).start()

    def finals(p):
        for way in (0, 1):
            for s, c in ((2, 2), (2, 3), (3, 0), (3, 1)):
                landed(p, way, s, c)
        for c in range(4):
            own(p, c).wait()

    def inner(p, first, last):
        def step(i, carry):
            rows = pl.ds(pl.multiple_of(i * TILE, TILE), TILE)
            left = halves(panel[p, :, :, rows].reshape(256, TILE))
            term = product(left, (high[rows, :], low[rows, :])).reshape(part.shape[1:])
            if first == 0:
                part[p] = jnp.where(i == 0, term, part[p] + term)
            else:
                part[p] += term
            return carry

        lax.fori_loop(first, last, step, 0)

    def turn(p, first, last):
        def step(i, carry):
            rows = pl.ds(pl.multiple_of(i * TILE, TILE), TILE)
            plain_high[rows, :], plain_low[rows, :] = halves(panel[p, :, :, rows].reshape(256, TILE).T)
            return carry

        lax.fori_loop(first, last, step, 0)

    def to_twin(p, which, source, target):
        return pltpu.make_async_remote_copy(
            src_ref=source, dst_ref=target, send_sem=core_send.at[p, which], recv_sem=core_recv.at[p, which],
            device_id=twin, device_id_type=MESH,
        )

    def exchange(p):
        return to_twin(p, 0, part.at[p, pl.ds((1 - core) * 16, 16)], pair.at[p])

    def scatter(p, k):
        return pltpu.make_async_remote_copy(
            src_ref=half.at[p, chip_at(k)], dst_ref=spread.at[p, k], send_sem=rs_send.at[p, k], recv_sem=rs_recv.at[p, k],
            device_id=chip_device(k), device_id_type=MESH,
        )

    def share(p, k):
        mine = sums.at[p, core * 16 + chip]
        return pltpu.make_async_remote_copy(
            src_ref=mine, dst_ref=mine, send_sem=ag_send.at[p, k], recv_sem=ag_recv.at[p, k],
            device_id=chip_device(k), device_id_type=MESH,
        )

    def shared(p, k):
        theirs = sums.at[p, core * 16 + ((y + 4 - k // 4) % 4) * 4 + (x + 4 - k % 4) % 4]
        return pltpu.make_async_remote_copy(
            src_ref=theirs, dst_ref=theirs, send_sem=ag_send.at[p, k], recv_sem=ag_recv.at[p, k],
            device_id=chip_device(k), device_id_type=MESH,
        )

    def each(action):
        def step(k, carry):
            action(k)
            return carry

        lax.fori_loop(1, 16, step, 0)

    def pair_sum(p):
        exchange(p).wait_recv()
        half[p] = part[p, pl.ds(core * 16, 16)] + pair[p]

    def chip_sum(p):
        each(lambda k: scatter(p, k).wait_recv())
        total = half[p, chip]
        for k in range(1, 16):
            total = total + spread[p, k]
        sums[p, core * 16 + chip] = total

    def join(p):
        each(lambda k: shared(p, k).wait_recv())
        mine = sums.at[p, pl.ds(core * 16, 16)]
        to_twin(p, 1, mine, mine).start()

    def coefficients(p):
        theirs = sums.at[p, pl.ds((1 - core) * 16, 16)]
        to_twin(p, 1, theirs, theirs).wait_recv()
        coef = jnp.dot(factors[p], sums[p].reshape(256, -1), precision=lax.Precision.HIGHEST, preferred_element_type=F32)
        coef_high[...], coef_low[...] = halves(coef)

    def update(p, last):
        def step(i, carry):
            rows = pl.ds(pl.multiple_of(i * TILE, TILE), TILE)
            fresh = field[rows, :] - product((plain_high[rows, :], plain_low[rows, :]), (coef_high[...], coef_low[...]))
            field[rows, :] = fresh
            if last:
                pltpu.make_async_copy(field.at[rows], out_ref.at[rows], out_sem.at[i]).start()
            else:
                high[rows, :], low[rows, :] = halves(fresh)
            return carry

        lax.fori_loop(0, blocks, step, 0)

    def chain(p, slot, last):
        finals(p)
        inner(p, 0, 3)
        slot(4, 5)
        inner(p, 3, 6)
        slot(5, 6)
        inner(p, 6, 8)
        exchange(p).start()
        slot(6, 7)
        pair_sum(p)
        each(lambda k: scatter(p, k).start())
        for i in range(4):
            turn(p, 2 * i, 2 * i + 2)
            slot(7 + i, 8 + i)
        chip_sum(p)
        each(lambda k: share(p, k).start())
        slot(11, 14)

    def finish(p, last):
        join(p)
        coefficients(p)
        update(p, last)

    load_factors.wait()
    slots(0, 0, 14)

    def turn_of_panel(p, carry):
        slots(p, 0, 4)

        @pl.when(p > 1)
        def _():
            finish(p - 2, False)

        chain(p - 1, functools.partial(slots, p), False)
        return carry

    lax.fori_loop(1, panels, turn_of_panel, 0)
    finish(panels - 2, False)
    chain(panels - 1, lambda first, last: None, True)
    finish(panels - 1, True)

    def drain(p, carry):
        for way in (0, 1):
            for i in range(14):
                hop(p, way, i // 4, i % 4).wait_send()
        exchange(p).wait_send()
        mine = sums.at[p, pl.ds(core * 16, 16)]
        to_twin(p, 1, mine, mine).wait_send()
        each(lambda k: scatter(p, k).wait_send())
        each(lambda k: share(p, k).wait_send())
        return carry

    lax.fori_loop(0, panels, drain, 0)

    def written(i, carry):
        rows = pl.ds(pl.multiple_of(i * TILE, TILE), TILE)
        pltpu.make_async_copy(field.at[rows], out_ref.at[rows], out_sem.at[i]).wait()
        return carry

    lax.fori_loop(0, blocks, written, 0)


def body(eigvecs, reflectors, t_factors):
    rows, columns = eigvecs.shape
    panels, block = t_factors.shape[:2]
    dma, vmem = pltpu.SemaphoreType.DMA, pltpu.VMEM
    return pl.pallas_call(
        kernel,
        out_shape=jax.ShapeDtypeStruct((rows, columns), F32),
        in_specs=[pl.BlockSpec(memory_space=pl.ANY)] * 3,
        out_specs=pl.BlockSpec(memory_space=pl.ANY),
        scratch_shapes=[
            vmem((panels, block // PIECE, PIECE, rows), F32),
            vmem((rows, columns), F32),
            vmem((rows, columns), BF16),
            vmem((rows, columns), BF16),
            vmem((rows, block), BF16),
            vmem((rows, block), BF16),
            vmem((panels, block, block), F32),
            vmem((block, columns), BF16),
            vmem((block, columns), BF16),
            vmem((panels, 32, 8, columns), F32),
            vmem((panels, 16, 8, columns), F32),
            vmem((panels, 16, 8, columns), F32),
            vmem((panels, 16, 8, columns), F32),
            vmem((panels, 32, 8, columns), F32),
            dma((panels, 2, 4, 4)),
            dma((panels, 2, 4, 4)),
            dma((panels, 16)),
            dma((panels, 16)),
            dma((panels, 16)),
            dma((panels, 16)),
            dma((panels, 2)),
            dma((panels, 2)),
            dma((panels, 4)),
            dma((2,)),
            dma((rows // TILE,)),
        ],
        compiler_params=pltpu.CompilerParams(collective_id=0, has_side_effects=True, vmem_limit_bytes=56 * 2**20),
        cost_estimate=pl.CostEstimate(flops=13 * 10**9, bytes_accessed=10 * 2**20, transcendentals=0),
    )(eigvecs, jnp.swapaxes(reflectors, 1, 2), t_factors)


def solution(mesh):
    in_specs = (P("rows", "cols"), P(None, "rows", "cols"), P())
    return jax.shard_map(body, mesh=mesh, in_specs=in_specs, out_specs=P("rows", "cols"), check_vma=False)
```

```python
import functools

import jax
import jax.numpy as jnp
from jax import lax
from jax.experimental import pallas as pl
from jax.experimental.pallas import tpu as pltpu
from jax.sharding import PartitionSpec as P

MESH = pl.DeviceIdType.MESH
F32, BF16 = jnp.float32, jnp.bfloat16
PIECE = 8
TILE = 256


def halves(value):
    high = value.astype(BF16)
    return high, (value - high.astype(F32)).astype(BF16)


def product(left, right):
    (left_high, left_low), (right_high, right_low) = left, right
    dot = functools.partial(jnp.dot, preferred_element_type=F32)
    return dot(left_high, right_high) + (dot(left_high, right_low) + dot(left_low, right_high))


def kernel(
    field_in, refl_in, factor_in,
    field, plain_high, plain_low, coef_high, coef_low,
    panel, high, low, factors,
    part, pair, half, spread, sums,
    z_send, z_recv, rs_send, rs_recv, ag_send, ag_recv, core_send, core_recv, own_sem, in_sem,
):
    row, z = lax.axis_index("rows"), lax.axis_index("cols")
    core, chip = row % 2, row // 2
    x, y = chip % 4, chip // 4
    z_next = ((row, (z + 1) % 8), (row, (z + 7) % 8))
    twin = (chip * 2 + 1 - core, z)

    def chip_at(k):
        return ((y + k // 4) % 4) * 4 + (x + k % 4) % 4

    def chip_device(k):
        return (chip_at(k) * 2 + core, z)

    panels, blocks = panel.shape[0], field.shape[0] // TILE

    load_field = pltpu.make_async_copy(field_in, field, in_sem.at[0])
    load_factors = pltpu.make_async_copy(factor_in, factors, in_sem.at[1])
    load_field.start()
    load_factors.start()

    def own(p, c):
        return pltpu.make_async_copy(refl_in.at[p, pl.ds(PIECE * c, PIECE)], panel.at[p, z * 4 + c], own_sem.at[p, c])

    for p in range(panels):
        for c in range(4):
            own(p, c).start()

    barrier = pltpu.get_barrier_semaphore()
    for device in (*z_next, twin):
        pl.semaphore_signal(barrier, inc=1, device_id=device, device_id_type=MESH)

    def greet(k, carry):
        pl.semaphore_signal(barrier, inc=1, device_id=chip_device(k), device_id_type=MESH)
        return carry

    lax.fori_loop(1, 16, greet, 0)
    def split(i, carry):
        rows = pl.ds(pl.multiple_of(i * TILE, TILE), TILE)
        high[rows, :], low[rows, :] = halves(field[rows, :])
        return carry

    pl.semaphore_wait(barrier, 18)

    def hop(p, way, s, c):
        c = c if way == 0 else 3 - c
        owner = (z + 8 - s) % 8 if way == 0 else (z + s) % 8
        source = refl_in.at[p, pl.ds(PIECE * c, PIECE)] if s == 0 else panel.at[p, owner * 4 + c]
        return pltpu.make_async_remote_copy(
            src_ref=source, dst_ref=panel.at[p, owner * 4 + c],
            send_sem=z_send.at[p, way, s, c], recv_sem=z_recv.at[p, way, s, c],
            device_id=z_next[way], device_id_type=MESH,
        )

    def landed(p, way, s, c):
        c = c if way == 0 else 3 - c
        owner = (z + 7 - s) % 8 if way == 0 else (z + 1 + s) % 8
        place = panel.at[p, owner * 4 + c]
        pltpu.make_async_remote_copy(
            src_ref=place, dst_ref=place,
            send_sem=z_send.at[p, way, s, c], recv_sem=z_recv.at[p, way, s, c],
            device_id=z_next[way], device_id_type=MESH,
        ).wait_recv()

    def slots(p, first, last, settle=True):
        for i in range(first, last):
            s, c = i // 4, i % 4
            for way in (0, 1):
                if s:
                    landed(p, way, s - 1, c)
                hop(p, way, s, c).start()
                if settle:
                    hop(p - 1, way, s, c).wait_send()

    def finals(p):
        for way in (0, 1):
            for s, c in ((2, 2), (2, 3), (3, 0), (3, 1)):
                landed(p, way, s, c)
        for c in range(4):
            own(p, c).wait()

    def inner(p, side):
        rows = pl.ds(side * 16, 16)
        total = 0.0
        for i in range(blocks):
            span = slice(i * TILE, (i + 1) * TILE)
            total += product(halves(panel[p, rows, :, span].reshape(128, TILE)), (high[span, :], low[span, :]))
        part[p, rows] = total.reshape(16, PIECE, -1)

    def turn(p, first, last):
        def step(i, carry):
            rows = pl.ds(pl.multiple_of(i * TILE, TILE), TILE)
            plain_high[rows, :], plain_low[rows, :] = halves(panel[p, :, :, rows].reshape(256, TILE).T)
            return carry

        lax.fori_loop(first, last, step, 0)

    def to_twin(p, which, source, target):
        return pltpu.make_async_remote_copy(
            src_ref=source, dst_ref=target, send_sem=core_send.at[p, which], recv_sem=core_recv.at[p, which],
            device_id=twin, device_id_type=MESH,
        )

    def exchange(p):
        return to_twin(p, 0, part.at[p, pl.ds((1 - core) * 16, 16)], pair.at[p])

    def scatter(p, k):
        return pltpu.make_async_remote_copy(
            src_ref=half.at[p, chip_at(k)], dst_ref=spread.at[p, k], send_sem=rs_send.at[p, k], recv_sem=rs_recv.at[p, k],
            device_id=chip_device(k), device_id_type=MESH,
        )

    def share(p, k):
        mine = sums.at[p, core * 16 + chip]
        return pltpu.make_async_remote_copy(
            src_ref=mine, dst_ref=mine, send_sem=ag_send.at[p, k], recv_sem=ag_recv.at[p, k],
            device_id=chip_device(k), device_id_type=MESH,
        )

    def shared(p, k):
        theirs = sums.at[p, core * 16 + ((y + 4 - k // 4) % 4) * 4 + (x + 4 - k % 4) % 4]
        return pltpu.make_async_remote_copy(
            src_ref=theirs, dst_ref=theirs, send_sem=ag_send.at[p, k], recv_sem=ag_recv.at[p, k],
            device_id=chip_device(k), device_id_type=MESH,
        )

    far_first = sorted(range(1, 16), key=lambda k: -min(k % 4, 4 - k % 4) - min(k // 4, 4 - k // 4))

    def each(action):
        for k in far_first:
            action(k)

    def pair_sum(p):
        exchange(p).wait_recv()
        half[p] = part[p, pl.ds(core * 16, 16)] + pair[p]

    def chip_sum(p):
        each(lambda k: scatter(p, k).wait_recv())
        total = half[p, chip]
        for k in range(1, 16):
            total = total + spread[p, k]
        sums[p, core * 16 + chip] = total

    def join(p):
        each(lambda k: shared(p, k).wait_recv())
        mine = sums.at[p, pl.ds(core * 16, 16)]
        to_twin(p, 1, mine, mine).start()
        each(lambda k: share(p, k).wait_send())

    def coefficients(p):
        theirs = sums.at[p, pl.ds((1 - core) * 16, 16)]
        to_twin(p, 1, theirs, theirs).wait()
        coef = product(halves(factors[p]), halves(sums[p].reshape(256, -1)))
        coef_high[...], coef_low[...] = halves(coef)

    def update():
        def step(i, carry):
            rows = pl.ds(pl.multiple_of(i * TILE, TILE), TILE)
            fresh = field[rows, :] - product((plain_high[rows, :], plain_low[rows, :]), (coef_high[...], coef_low[...]))
            field[rows, :] = fresh
            high[rows, :], low[rows, :] = halves(fresh)
            return carry

        lax.fori_loop(0, blocks, step, 0, unroll=4)

    def chain(p, slot):
        finals(p)
        inner(p, 1 - core)
        exchange(p).start()
        slot(4, 5)
        inner(p, core)
        slot(5, 6)
        pair_sum(p)
        each(lambda k: scatter(p, k).start())
        exchange(p).wait_send()
        turn(p, 0, 4)
        slot(6, 7)
        turn(p, 4, 8)
        slot(7, 10)
        chip_sum(p)
        each(lambda k: share(p, k).start())
        each(lambda k: scatter(p, k).wait_send())
        slot(10, 14)

    def finish(p):
        join(p)
        coefficients(p)

    slots(0, 0, 4, False)
    load_field.wait()
    lax.fori_loop(0, blocks, split, 0)
    load_factors.wait()
    slots(0, 4, 14, False)

    def turn_of_panel(p, carry):
        slots(p, 0, 4)

        @pl.when(p > 1)
        def _():
            finish(p - 2)
            update()

        chain(p - 1, functools.partial(slots, p))
        return carry

    lax.fori_loop(1, panels, turn_of_panel, 0)
    finish(panels - 2)
    update()

    def settle_last(first, last):
        for i in range(first - 4, last - 4 if last < 14 else 14):
            for way in (0, 1):
                hop(panels - 1, way, i // 4, i % 4).wait_send()

    chain(panels - 1, settle_last)
    finish(panels - 1)


def last_update(field, plain_high, plain_low, coef_high, coef_low, out_ref, held, out_sem):
    copies = []
    for i in range(held.shape[0]):
        rows = slice(i * TILE, (i + 1) * TILE)
        held[i] = field[rows, :] - product((plain_high[rows, :], plain_low[rows, :]), (coef_high[...], coef_low[...]))
        copies.append(pltpu.make_async_copy(held.at[i], out_ref.at[rows], out_sem.at[i]))
        copies[i].start()
    for copy in copies:
        copy.wait()


def body(eigvecs, reflectors, t_factors):
    rows, columns = eigvecs.shape
    panels, block = t_factors.shape[:2]
    dma, vmem = pltpu.SemaphoreType.DMA, pltpu.VMEM
    shapes = [((rows, columns), F32), ((rows, block), BF16), ((rows, block), BF16), ((block, columns), BF16), ((block, columns), BF16)]
    parts = pl.pallas_call(
        kernel,
        out_shape=[vmem(*shape) for shape in shapes],
        in_specs=[pl.BlockSpec(memory_space=pltpu.HBM)] * 3,
        out_specs=[pl.BlockSpec(memory_space=vmem)] * 5,
        scratch_shapes=[
            vmem((panels, block // PIECE, PIECE, rows), F32),
            vmem((rows, columns), BF16),
            vmem((rows, columns), BF16),
            vmem((panels, block, block), F32),
            vmem((panels, 32, 8, columns), F32),
            vmem((panels, 16, 8, columns), F32),
            vmem((panels, 16, 8, columns), F32),
            vmem((panels, 16, 8, columns), F32),
            vmem((panels, 32, 8, columns), F32),
            dma((panels, 2, 4, 4)),
            dma((panels, 2, 4, 4)),
            dma((panels, 16)),
            dma((panels, 16)),
            dma((panels, 16)),
            dma((panels, 16)),
            dma((panels, 2)),
            dma((panels, 2)),
            dma((panels, 4)),
            dma((2,)),
        ],
        compiler_params=pltpu.CompilerParams(collective_id=0, has_side_effects=True, vmem_limit_bytes=48 * 2**20),
        cost_estimate=pl.CostEstimate(flops=12 * 10**9, bytes_accessed=6 * 2**20, transcendentals=0),
    )(*(pltpu.with_memory_space_constraint(a, pltpu.HBM) for a in (eigvecs, jnp.swapaxes(reflectors, 1, 2), t_factors)))
    return pl.pallas_call(
        last_update,
        out_shape=jax.ShapeDtypeStruct((rows, columns), F32),
        in_specs=[pl.BlockSpec(memory_space=vmem)] * 5,
        out_specs=pl.BlockSpec(memory_space=pl.ANY),
        scratch_shapes=[vmem((rows // TILE, TILE, columns), F32), dma((rows // TILE,))],
        compiler_params=pltpu.CompilerParams(vmem_limit_bytes=16 * 2**20),
        cost_estimate=pl.CostEstimate(flops=2 * 10**9, bytes_accessed=4 * 2**20, transcendentals=0),
    )(*parts)


def solution(mesh):
    in_specs = (P("rows", "cols"), P(None, "rows", "cols"), P())
    return jax.shard_map(body, mesh=mesh, in_specs=in_specs, out_specs=P("rows", "cols"), check_vma=False)
```

```python
import functools

import jax
import jax.numpy as jnp
from jax import lax
from jax.experimental import pallas as pl
from jax.experimental.pallas import tpu as pltpu
from jax.sharding import PartitionSpec as P

MESH = pl.DeviceIdType.MESH
F32, BF16 = jnp.float32, jnp.bfloat16
PIECE = 8
TILE = 256


def halves(value):
    high = value.astype(BF16)
    return high, (value - high.astype(F32)).astype(BF16)


def product(left, right):
    (left_high, left_low), (right_high, right_low) = left, right
    dot = functools.partial(jnp.dot, preferred_element_type=F32)
    return dot(left_high, right_high) + (dot(left_high, right_low) + dot(left_low, right_high))


def kernel(
    field_in, refl_in, factor_in,
    field, plain_high, plain_low, coef_high, coef_low,
    panel, high, low, factors,
    part, pair, half, spread, sums,
    z_send, z_recv, rs_send, rs_recv, ag_send, ag_recv, core_send, core_recv, own_sem, in_sem, ready,
):
    row, z = lax.axis_index("rows"), lax.axis_index("cols")
    core, chip = lax.rem(row, 2), row // 2
    x, y = lax.rem(chip, 4), chip // 4
    z_next = ((row, lax.rem(z + 1, 8)), (row, lax.rem(z + 7, 8)))
    twin = (chip * 2 + 1 - core, z)

    def chip_at(k):
        return lax.rem(y + k // 4, 4) * 4 + lax.rem(x + k % 4, 4)

    def chip_device(k):
        return (chip_at(k) * 2 + core, z)

    panels, blocks = panel.shape[0], field.shape[0] // TILE

    load_field = pltpu.make_async_copy(field_in, field, in_sem.at[0])
    load_factors = pltpu.make_async_copy(factor_in, factors, in_sem.at[1])
    load_field.start()
    load_factors.start()

    def own(p, c):
        return pltpu.make_async_copy(refl_in.at[p, pl.ds(PIECE * c, PIECE)], panel.at[p, z * 4 + c], own_sem.at[p, c])

    for p in range(panels):
        for c in range(4):
            own(p, c).start()

    barrier = pltpu.get_barrier_semaphore()
    beside = [chip_device(k) for k in (1, 3, 4, 12)]
    for device in (*z_next, twin, *beside):
        pl.semaphore_signal(barrier, inc=1, device_id=device, device_id_type=MESH)

    def tell(stage):
        for device in beside:
            pl.semaphore_signal(ready.at[stage], inc=1, device_id=device, device_id_type=MESH)

    def hear(stage):
        pl.semaphore_wait(ready.at[stage], len(beside))

    def split(i, carry):
        rows = pl.ds(pl.multiple_of(i * TILE, TILE), TILE)
        high[rows, :], low[rows, :] = halves(field[rows, :])
        return carry

    pl.semaphore_wait(barrier, 7)

    def hop(p, way, s, c):
        c = c if way == 0 else 3 - c
        owner = lax.rem(z + (8 - s if way == 0 else s), 8)
        source = refl_in.at[p, pl.ds(PIECE * c, PIECE)] if s == 0 else panel.at[p, owner * 4 + c]
        return pltpu.make_async_remote_copy(
            src_ref=source, dst_ref=panel.at[p, owner * 4 + c],
            send_sem=z_send.at[p, way, s, c], recv_sem=z_recv.at[p, way, s, c],
            device_id=z_next[way], device_id_type=MESH,
        )

    def landed(p, way, s, c):
        c = c if way == 0 else 3 - c
        owner = lax.rem(z + (7 - s if way == 0 else 1 + s), 8)
        place = panel.at[p, owner * 4 + c]
        pltpu.make_async_remote_copy(
            src_ref=place, dst_ref=place,
            send_sem=z_send.at[p, way, s, c], recv_sem=z_recv.at[p, way, s, c],
            device_id=z_next[way], device_id_type=MESH,
        ).wait_recv()

    def slots(p, first, last, settle=True):
        for i in range(first, last):
            s, c = i // 4, i % 4
            for way in (0, 1):
                if s:
                    landed(p, way, s - 1, c)
                hop(p, way, s, c).start()
                if settle:
                    hop(p - 1, way, s, c).wait_send()

    def finals(p):
        for way in (0, 1):
            for s, c in ((2, 2), (2, 3), (3, 0), (3, 1)):
                landed(p, way, s, c)
        for c in range(4):
            own(p, c).wait()

    def inner(p, side):
        rows = pl.ds(side * 16, 16)
        total = 0.0
        for i in range(blocks):
            span = slice(i * TILE, (i + 1) * TILE)
            total += product(halves(panel[p, rows, :, span].reshape(128, TILE)), (high[span, :], low[span, :]))
        part[p, rows] = total.reshape(16, PIECE, -1)

    def turn(p, first, last):
        def step(i, carry):
            rows = pl.ds(pl.multiple_of(i * TILE, TILE), TILE)
            plain_high[rows, :], plain_low[rows, :] = halves(panel[p, :, :, rows].reshape(256, TILE).T)
            return carry

        lax.fori_loop(first, last, step, 0)

    def to_twin(p, which, source, target):
        return pltpu.make_async_remote_copy(
            src_ref=source, dst_ref=target, send_sem=core_send.at[p, which], recv_sem=core_recv.at[p, which],
            device_id=twin, device_id_type=MESH,
        )

    def exchange(p):
        return to_twin(p, 0, part.at[p, pl.ds((1 - core) * 16, 16)], pair.at[p])

    def scatter(p, k):
        return pltpu.make_async_remote_copy(
            src_ref=half.at[p, chip_at(k)], dst_ref=spread.at[p, k], send_sem=rs_send.at[p, k], recv_sem=rs_recv.at[p, k],
            device_id=chip_device(k), device_id_type=MESH,
        )

    def share(p, k):
        mine = sums.at[p, core * 16 + chip]
        return pltpu.make_async_remote_copy(
            src_ref=mine, dst_ref=mine, send_sem=ag_send.at[p, k], recv_sem=ag_recv.at[p, k],
            device_id=chip_device(k), device_id_type=MESH,
        )

    def shared(p, k):
        theirs = sums.at[p, core * 16 + chip_at((4 - k // 4) % 4 * 4 + (4 - k % 4) % 4)]
        return pltpu.make_async_remote_copy(
            src_ref=theirs, dst_ref=theirs, send_sem=ag_send.at[p, k], recv_sem=ag_recv.at[p, k],
            device_id=chip_device(k), device_id_type=MESH,
        )

    far_first = sorted(range(1, 16), key=lambda k: -min(k % 4, 4 - k % 4) - min(k // 4, 4 - k // 4))

    def each(action):
        for k in far_first:
            action(k)

    def pair_sum(p):
        exchange(p).wait_recv()
        half[p] = part[p, pl.ds(core * 16, 16)] + pair[p]

    def chip_sum(p):
        each(lambda k: scatter(p, k).wait_recv())
        total = half[p, chip]
        for k in range(1, 16):
            total = total + spread[p, k]
        sums[p, core * 16 + chip] = total

    def join(p):
        each(lambda k: shared(p, k).wait_recv())
        mine = sums.at[p, pl.ds(core * 16, 16)]
        to_twin(p, 1, mine, mine).start()
        each(lambda k: share(p, k).wait_send())

    def coefficients(p):
        def term(side):
            rows, columns = pl.ds(side * 16, 16), pl.ds(pl.multiple_of(side * 128, 128), 128)
            return product(halves(factors[p, :, columns]), halves(sums[p, rows].reshape(128, -1)))

        coef = term(core)
        theirs = sums.at[p, pl.ds((1 - core) * 16, 16)]
        to_twin(p, 1, theirs, theirs).wait()
        coef_high[...], coef_low[...] = halves(coef + term(1 - core))

    def update():
        def step(i, carry):
            rows = pl.ds(pl.multiple_of(i * TILE, TILE), TILE)
            fresh = field[rows, :] - product((plain_high[rows, :], plain_low[rows, :]), (coef_high[...], coef_low[...]))
            field[rows, :] = fresh
            high[rows, :], low[rows, :] = halves(fresh)
            return carry

        lax.fori_loop(0, blocks, step, 0, unroll=4)

    def chain(p, slot):
        finals(p)
        inner(p, 1 - core)
        exchange(p).start()
        slot(4, 5)
        inner(p, core)
        slot(5, 6)
        pair_sum(p)
        each(lambda k: scatter(p, k).start())
        exchange(p).wait_send()
        turn(p, 0, 4)
        slot(6, 7)
        turn(p, 4, 8)
        slot(7, 10)
        chip_sum(p)
        each(lambda k: share(p, k).start())
        each(lambda k: scatter(p, k).wait_send())
        slot(10, 14)

    def finish(p):
        join(p)
        coefficients(p)

    slots(0, 0, 4, False)
    load_field.wait()
    lax.fori_loop(0, blocks, split, 0)
    load_factors.wait()
    for stage in range(3):
        tell(stage)
        slots(0, 4 + 2 * stage, 6 + 2 * stage, False)
        hear(stage)
    slots(0, 10, 14, False)

    def turn_of_panel(p, carry):
        slots(p, 0, 4)

        @pl.when(p > 1)
        def _():
            finish(p - 2)
            update()

        chain(p - 1, functools.partial(slots, p))
        return carry

    lax.fori_loop(1, panels, turn_of_panel, 0)
    finish(panels - 2)
    update()

    def settle_last(first, last):
        for i in range(first - 4, last - 4 if last < 14 else 14):
            for way in (0, 1):
                hop(panels - 1, way, i // 4, i % 4).wait_send()

    chain(panels - 1, settle_last)
    finish(panels - 1)


def last_update(field, plain_high, plain_low, coef_high, coef_low, out_ref, held, out_sem):
    copies = []
    for i in range(held.shape[0]):
        rows = slice(i * TILE, (i + 1) * TILE)
        held[i] = field[rows, :] - product((plain_high[rows, :], plain_low[rows, :]), (coef_high[...], coef_low[...]))
        copies.append(pltpu.make_async_copy(held.at[i], out_ref.at[rows], out_sem.at[i]))
        copies[i].start()
    for copy in copies:
        copy.wait()


def body(eigvecs, reflectors, t_factors):
    rows, columns = eigvecs.shape
    panels, block = t_factors.shape[:2]
    dma, vmem = pltpu.SemaphoreType.DMA, pltpu.VMEM
    shapes = [((rows, columns), F32), ((rows, block), BF16), ((rows, block), BF16), ((block, columns), BF16), ((block, columns), BF16)]
    parts = pl.pallas_call(
        kernel,
        out_shape=[vmem(*shape) for shape in shapes],
        in_specs=[pl.BlockSpec(memory_space=pltpu.HBM)] * 3,
        out_specs=[pl.BlockSpec(memory_space=vmem)] * 5,
        scratch_shapes=[
            vmem((panels, block // PIECE, PIECE, rows), F32),
            vmem((rows, columns), BF16),
            vmem((rows, columns), BF16),
            vmem((panels, block, block), F32),
            vmem((panels, 32, 8, columns), F32),
            vmem((panels, 16, 8, columns), F32),
            vmem((panels, 16, 8, columns), F32),
            vmem((panels, 16, 8, columns), F32),
            vmem((panels, 32, 8, columns), F32),
            dma((panels, 2, 4, 4)),
            dma((panels, 2, 4, 4)),
            dma((panels, 16)),
            dma((panels, 16)),
            dma((panels, 16)),
            dma((panels, 16)),
            dma((panels, 2)),
            dma((panels, 2)),
            dma((panels, 4)),
            dma((2,)),
            pltpu.SemaphoreType.REGULAR((3,)),
        ],
        compiler_params=pltpu.CompilerParams(collective_id=0, has_side_effects=True, vmem_limit_bytes=48 * 2**20),
        cost_estimate=pl.CostEstimate(flops=12 * 10**9, bytes_accessed=6 * 2**20, transcendentals=0),
    )(*(pltpu.with_memory_space_constraint(a, pltpu.HBM) for a in (eigvecs, jnp.swapaxes(reflectors, 1, 2), t_factors)))
    return pl.pallas_call(
        last_update,
        out_shape=jax.ShapeDtypeStruct((rows, columns), F32),
        in_specs=[pl.BlockSpec(memory_space=vmem)] * 5,
        out_specs=pl.BlockSpec(memory_space=pl.ANY),
        scratch_shapes=[vmem((rows // TILE, TILE, columns), F32), dma((rows // TILE,))],
        compiler_params=pltpu.CompilerParams(vmem_limit_bytes=16 * 2**20),
        cost_estimate=pl.CostEstimate(flops=2 * 10**9, bytes_accessed=4 * 2**20, transcendentals=0),
    )(*parts)


def solution(mesh):
    in_specs = (P("rows", "cols"), P(None, "rows", "cols"), P())
    return jax.shard_map(body, mesh=mesh, in_specs=in_specs, out_specs=P("rows", "cols"), check_vma=False)
```

```python
import functools

import jax
import jax.numpy as jnp
from jax import lax
from jax.experimental import pallas as pl
from jax.experimental.pallas import tpu as pltpu
from jax.sharding import PartitionSpec as P

MESH = pl.DeviceIdType.MESH
F32, BF16 = jnp.float32, jnp.bfloat16
PIECE = 8
TILE = 256


def halves(value):
    high = value.astype(BF16)
    return high, (value - high.astype(F32)).astype(BF16)


def product(left, right):
    (left_high, left_low), (right_high, right_low) = left, right
    dot = functools.partial(jnp.dot, preferred_element_type=F32)
    return dot(left_high, right_high) + (dot(left_high, right_low) + dot(left_low, right_high))


def kernel(
    field_in, refl_in, factor_in,
    field, plain_high, plain_low, coef_high, coef_low,
    panel, high, low, factors,
    part, pair, half, spread, sums,
    z_send, z_recv, rs_send, rs_recv, ag_send, ag_recv, core_send, core_recv, in_sem, ready,
):
    row, z = lax.axis_index("rows"), lax.axis_index("cols")
    core, chip = lax.rem(row, 2), row // 2
    x, y = lax.rem(chip, 4), chip // 4
    z_next = ((row, lax.rem(z + 1, 8)), (row, lax.rem(z + 7, 8)))
    twin = (chip * 2 + 1 - core, z)

    def chip_at(k):
        return lax.rem(y + k // 4, 4) * 4 + lax.rem(x + k % 4, 4)

    def chip_device(k):
        return (chip_at(k) * 2 + core, z)

    panels, blocks = panel.shape[0], field.shape[0] // TILE

    barrier = pltpu.get_barrier_semaphore()
    beside = [chip_device(k) for k in (1, 3, 4, 12)]
    for device in (*z_next, twin, *beside):
        pl.semaphore_signal(barrier, inc=1, device_id=device, device_id_type=MESH)

    def tell(stage):
        for device in beside:
            pl.semaphore_signal(ready.at[stage], inc=1, device_id=device, device_id_type=MESH)

    def hear(stage):
        pl.semaphore_wait(ready.at[stage], len(beside))

    def split(i, carry):
        rows = pl.ds(pl.multiple_of(i * TILE, TILE), TILE)
        high[rows, :], low[rows, :] = halves(field[rows, :])
        return carry


    load_field = pltpu.make_async_copy(field_in, field, in_sem.at[0])
    load_factors = pltpu.make_async_copy(factor_in, factors, in_sem.at[1])
    load_own = pltpu.make_async_copy(refl_in, panel.at[:, pl.ds(z * 4, 4)], in_sem.at[2])
    load_field.start()
    pl.semaphore_wait(barrier, 7)

    def hop(p, way, s, c):
        c = c if way == 0 else 3 - c
        owner = lax.rem(z + (8 - s if way == 0 else s), 8)
        source = refl_in.at[p, c] if s == 0 else panel.at[p, owner * 4 + c]
        return pltpu.make_async_remote_copy(
            src_ref=source, dst_ref=panel.at[p, owner * 4 + c],
            send_sem=z_send.at[p, way, s, c], recv_sem=z_recv.at[p, way, s, c],
            device_id=z_next[way], device_id_type=MESH,
        )

    def landed(p, way, s, c):
        c = c if way == 0 else 3 - c
        owner = lax.rem(z + (7 - s if way == 0 else 1 + s), 8)
        place = panel.at[p, owner * 4 + c]
        pltpu.make_async_remote_copy(
            src_ref=place, dst_ref=place,
            send_sem=z_send.at[p, way, s, c], recv_sem=z_recv.at[p, way, s, c],
            device_id=z_next[way], device_id_type=MESH,
        ).wait_recv()

    def slots(p, first, last, settle=True):
        for i in range(first, last):
            s, c = i // 4, i % 4
            for way in (0, 1):
                if s:
                    landed(p, way, s - 1, c)
                hop(p, way, s, c).start()
                if settle:
                    hop(p - 1, way, s, c).wait_send()

    def finals(p):
        for way in (0, 1):
            for s, c in ((2, 2), (2, 3), (3, 0), (3, 1)):
                landed(p, way, s, c)

    def inner(p, side):
        rows = pl.ds(side * 16, 16)
        total = 0.0
        for i in range(blocks):
            span = slice(i * TILE, (i + 1) * TILE)
            total += product(halves(panel[p, rows, :, span].reshape(128, TILE)), (high[span, :], low[span, :]))
        part[p, rows] = total.reshape(16, PIECE, -1)

    def turn(p, first, last):
        def step(i, carry):
            rows = pl.ds(pl.multiple_of(i * TILE, TILE), TILE)
            plain_high[rows, :], plain_low[rows, :] = halves(panel[p, :, :, rows].reshape(256, TILE).T)
            return carry

        lax.fori_loop(first, last, step, 0)

    def to_twin(p, which, source, target):
        return pltpu.make_async_remote_copy(
            src_ref=source, dst_ref=target, send_sem=core_send.at[p, which], recv_sem=core_recv.at[p, which],
            device_id=twin, device_id_type=MESH,
        )

    def exchange(p):
        return to_twin(p, 0, part.at[p, pl.ds((1 - core) * 16, 16)], pair.at[p])

    def scatter(p, k):
        return pltpu.make_async_remote_copy(
            src_ref=half.at[p, chip_at(k)], dst_ref=spread.at[p, k - 1], send_sem=rs_send.at[p], recv_sem=rs_recv.at[p],
            device_id=chip_device(k), device_id_type=MESH,
        )

    def share(p, k):
        mine = sums.at[p, core * 16 + chip]
        return pltpu.make_async_remote_copy(
            src_ref=mine, dst_ref=mine, send_sem=ag_send.at[p], recv_sem=ag_recv.at[p],
            device_id=chip_device(k), device_id_type=MESH,
        )

    def all_scattered(p):
        whole = spread.at[p]
        return pltpu.make_async_remote_copy(
            src_ref=whole, dst_ref=whole, send_sem=rs_send.at[p], recv_sem=rs_recv.at[p], device_id=twin, device_id_type=MESH
        )

    def all_shared(p):
        whole = sums.at[p, pl.ds(0, 15)]
        return pltpu.make_async_remote_copy(
            src_ref=whole, dst_ref=whole, send_sem=ag_send.at[p], recv_sem=ag_recv.at[p], device_id=twin, device_id_type=MESH
        )

    far_first = sorted(range(1, 16), key=lambda k: -min(k % 4, 4 - k % 4) - min(k // 4, 4 - k // 4))

    def each(action):
        for k in far_first:
            action(k)

    def pair_sum(p):
        exchange(p).wait_recv()
        half[p] = part[p, pl.ds(core * 16, 16)] + pair[p]

    def chip_sum(p):
        all_scattered(p).wait_recv()
        total = half[p, chip]
        for k in range(15):
            total = total + spread[p, k]
        sums[p, core * 16 + chip] = total

    def join(p):
        all_shared(p).wait_recv()
        mine = sums.at[p, pl.ds(core * 16, 16)]
        to_twin(p, 1, mine, mine).start()
        all_shared(p).wait_send()

    def coefficients(p):
        def term(side):
            rows, columns = pl.ds(side * 16, 16), pl.ds(pl.multiple_of(side * 128, 128), 128)
            return product(halves(factors[p, :, columns]), halves(sums[p, rows].reshape(128, -1)))

        coef = term(core)
        theirs = sums.at[p, pl.ds((1 - core) * 16, 16)]
        to_twin(p, 1, theirs, theirs).wait()
        coef_high[...], coef_low[...] = halves(coef + term(1 - core))

    def update():
        def step(i, carry):
            rows = pl.ds(pl.multiple_of(i * TILE, TILE), TILE)
            fresh = field[rows, :] - product((plain_high[rows, :], plain_low[rows, :]), (coef_high[...], coef_low[...]))
            field[rows, :] = fresh
            high[rows, :], low[rows, :] = halves(fresh)
            return carry

        lax.fori_loop(0, blocks, step, 0, unroll=4)

    def chain(p, slot):
        finals(p)
        inner(p, 1 - core)
        exchange(p).start()
        slot(4, 5)
        inner(p, core)
        slot(5, 6)
        pair_sum(p)
        each(lambda k: scatter(p, k).start())
        exchange(p).wait_send()
        turn(p, 0, 4)
        slot(6, 7)
        turn(p, 4, 8)
        slot(7, 10)
        chip_sum(p)
        each(lambda k: share(p, k).start())
        all_scattered(p).wait_send()
        slot(10, 14)

    def finish(p):
        join(p)
        coefficients(p)

    slots(0, 0, 4, False)
    load_own.start()
    load_factors.start()
    load_field.wait()
    lax.fori_loop(0, blocks, split, 0)
    load_factors.wait()
    for stage in range(3):
        tell(stage)
        slots(0, 4 + 2 * stage, 6 + 2 * stage, False)
        hear(stage)
    slots(0, 10, 14, False)
    load_own.wait()

    def turn_of_panel(p, carry):
        slots(p, 0, 4)

        @pl.when(p > 1)
        def _():
            finish(p - 2)
            update()

        chain(p - 1, functools.partial(slots, p))
        return carry

    lax.fori_loop(1, panels, turn_of_panel, 0)
    finish(panels - 2)
    update()

    def settle_last(first, last):
        for i in range(first - 4, last - 4 if last < 14 else 14):
            for way in (0, 1):
                hop(panels - 1, way, i // 4, i % 4).wait_send()

    chain(panels - 1, settle_last)
    finish(panels - 1)


def last_update(field, plain_high, plain_low, coef_high, coef_low, out_ref, held, out_sem):
    copies = []
    for i in range(held.shape[0]):
        rows = slice(i * TILE, (i + 1) * TILE)
        held[i] = field[rows, :] - product((plain_high[rows, :], plain_low[rows, :]), (coef_high[...], coef_low[...]))
        copies.append(pltpu.make_async_copy(held.at[i], out_ref.at[rows], out_sem.at[i]))
        copies[i].start()
    for copy in copies:
        copy.wait()


def body(eigvecs, reflectors, t_factors):
    rows, columns = eigvecs.shape
    panels, block = t_factors.shape[:2]
    dma, vmem = pltpu.SemaphoreType.DMA, pltpu.VMEM
    shapes = [((rows, columns), F32), ((rows, block), BF16), ((rows, block), BF16), ((block, columns), BF16), ((block, columns), BF16)]
    own = jnp.swapaxes(reflectors, 1, 2).reshape(panels, -1, PIECE, rows)
    parts = pl.pallas_call(
        kernel,
        out_shape=[vmem(*shape) for shape in shapes],
        in_specs=[pl.BlockSpec(memory_space=pltpu.HBM)] * 3,
        out_specs=[pl.BlockSpec(memory_space=vmem)] * 5,
        scratch_shapes=[
            vmem((panels, block // PIECE, PIECE, rows), F32),
            vmem((rows, columns), BF16),
            vmem((rows, columns), BF16),
            vmem((panels, block, block), F32),
            vmem((panels, 32, 8, columns), F32),
            vmem((panels, 16, 8, columns), F32),
            vmem((panels, 16, 8, columns), F32),
            vmem((panels, 15, 8, columns), F32),
            vmem((panels, 32, 8, columns), F32),
            dma((panels, 2, 4, 4)),
            dma((panels, 2, 4, 4)),
            dma((panels,)),
            dma((panels,)),
            dma((panels,)),
            dma((panels,)),
            dma((panels, 2)),
            dma((panels, 2)),
            dma((3,)),
            pltpu.SemaphoreType.REGULAR((3,)),
        ],
        compiler_params=pltpu.CompilerParams(collective_id=0, has_side_effects=True, vmem_limit_bytes=48 * 2**20),
        cost_estimate=pl.CostEstimate(flops=12 * 10**9, bytes_accessed=6 * 2**20, transcendentals=0),
    )(*(pltpu.with_memory_space_constraint(a, pltpu.HBM) for a in (eigvecs, own, t_factors)))
    return pl.pallas_call(
        last_update,
        out_shape=jax.ShapeDtypeStruct((rows, columns), F32),
        in_specs=[pl.BlockSpec(memory_space=vmem)] * 5,
        out_specs=pl.BlockSpec(memory_space=pl.ANY),
        scratch_shapes=[vmem((rows // TILE, TILE, columns), F32), dma((rows // TILE,))],
        compiler_params=pltpu.CompilerParams(vmem_limit_bytes=16 * 2**20),
        cost_estimate=pl.CostEstimate(flops=2 * 10**9, bytes_accessed=4 * 2**20, transcendentals=0),
    )(*parts)


def solution(mesh):
    in_specs = (P("rows", "cols"), P(None, "rows", "cols"), P())
    return jax.shard_map(body, mesh=mesh, in_specs=in_specs, out_specs=P("rows", "cols"), check_vma=False)
```

```python
import functools

import jax
import jax.numpy as jnp
from jax import lax
from jax.experimental import pallas as pl
from jax.experimental.pallas import tpu as pltpu
from jax.sharding import PartitionSpec as P

MESH = pl.DeviceIdType.MESH
F32, BF16 = jnp.float32, jnp.bfloat16
PIECE = 8
TILE = 256


def halves(value):
    high = value.astype(BF16)
    return high, (value - high.astype(F32)).astype(BF16)


def product(left, right):
    (left_high, left_low), (right_high, right_low) = left, right
    dot = functools.partial(jnp.dot, preferred_element_type=F32)
    return dot(left_high, right_high) + (dot(left_high, right_low) + dot(left_low, right_high))


def kernel(
    field_in, refl_in, factor_in,
    field, plain_high, plain_low, coef_high, coef_low,
    panel, high, low, factors,
    part, pair, half, spread, sums,
    z_send, z_recv, rs_send, rs_recv, ag_send, ag_recv, core_send, core_recv, in_sem, ready,
):
    row, z = lax.axis_index("rows"), lax.axis_index("cols")
    core, chip = lax.rem(row, 2), row // 2
    x, y = lax.rem(chip, 4), chip // 4
    z_next = ((row, lax.rem(z + 1, 8)), (row, lax.rem(z + 7, 8)))
    twin = (chip * 2 + 1 - core, z)

    def chip_at(k):
        return lax.rem(y + k // 4, 4) * 4 + lax.rem(x + k % 4, 4)

    def chip_device(k):
        return (chip_at(k) * 2 + core, z)

    panels, blocks = panel.shape[0], field.shape[0] // TILE

    barrier = pltpu.get_barrier_semaphore()
    beside = [chip_device(k) for k in (1, 3, 4, 12)]
    for device in (*z_next, twin, *beside):
        pl.semaphore_signal(barrier, inc=1, device_id=device, device_id_type=MESH)

    def tell(stage):
        for device in beside:
            pl.semaphore_signal(ready.at[stage], inc=1, device_id=device, device_id_type=MESH)

    def hear(stage):
        pl.semaphore_wait(ready.at[stage], len(beside))

    def split(i, carry):
        rows = pl.ds(pl.multiple_of(i * TILE, TILE), TILE)
        high[rows, :], low[rows, :] = halves(field[rows, :])
        return carry


    load_field = pltpu.make_async_copy(field_in, field, in_sem.at[0])
    load_factors = pltpu.make_async_copy(factor_in, factors, in_sem.at[1])
    load_own = pltpu.make_async_copy(refl_in, panel.at[:, pl.ds(z * 4, 4)], in_sem.at[2])
    load_field.start()
    pl.semaphore_wait(barrier, 7)

    def move(p, way, owner, c, step, source=None):
        piece = c if way == 0 else 3 - c
        place = panel.at[p, lax.rem(owner, 8) * 4 + piece]
        return pltpu.make_async_remote_copy(
            src_ref=place if source is None else source.at[p, piece], dst_ref=place, send_sem=z_send.at[p, way],
            recv_sem=z_recv.at[p, way, step * 4 + c if step < 2 or (step == 2 and c < 2) else 10],
            device_id=z_next[way], device_id_type=MESH,
        )

    def hop(p, way, s, c):
        return move(p, way, z + (8 - s if way == 0 else s), c, s, refl_in if s == 0 else None)

    def landed(p, way, s, c):
        move(p, way, z + (7 - s if way == 0 else 1 + s), c, s).wait_recv()

    def many(p, way, count):
        places = panel.at[p, pl.ds(0, count)]
        return pltpu.make_async_remote_copy(
            src_ref=places, dst_ref=places, send_sem=z_send.at[p, way], recv_sem=z_recv.at[p, way, 10],
            device_id=z_next[way], device_id_type=MESH,
        )

    def slots(p, first, last):
        for i in range(first, last):
            s, c = i // 4, i % 4
            for way in (0, 1):
                if s:
                    landed(p, way, s - 1, c)
                hop(p, way, s, c).start()

    def sent(p):
        for way in (0, 1):
            many(p, way, 14).wait_send()

    def finals(p):
        for way in (0, 1):
            many(p, way, 4).wait_recv()

    def inner(p, side):
        rows = pl.ds(side * 16, 16)
        total = 0.0
        for i in range(blocks):
            span = slice(i * TILE, (i + 1) * TILE)
            total += product(halves(panel[p, rows, :, span].reshape(128, TILE)), (high[span, :], low[span, :]))
        part[p, rows] = total.reshape(16, PIECE, -1)

    def turn(p, first, last):
        def step(i, carry):
            rows = pl.ds(pl.multiple_of(i * TILE, TILE), TILE)
            plain_high[rows, :], plain_low[rows, :] = halves(panel[p, :, :, rows].reshape(256, TILE).T)
            return carry

        lax.fori_loop(first, last, step, 0)

    def to_twin(p, which, source, target):
        return pltpu.make_async_remote_copy(
            src_ref=source, dst_ref=target, send_sem=core_send.at[p, which], recv_sem=core_recv.at[p, which],
            device_id=twin, device_id_type=MESH,
        )

    def exchange(p):
        return to_twin(p, 0, part.at[p, pl.ds((1 - core) * 16, 16)], pair.at[p])

    def scatter(p, k):
        return pltpu.make_async_remote_copy(
            src_ref=half.at[p, chip_at(k)], dst_ref=spread.at[p, k - 1], send_sem=rs_send.at[p], recv_sem=rs_recv.at[p],
            device_id=chip_device(k), device_id_type=MESH,
        )

    def share(p, k):
        mine = sums.at[p, core * 16 + chip]
        return pltpu.make_async_remote_copy(
            src_ref=mine, dst_ref=mine, send_sem=ag_send.at[p], recv_sem=ag_recv.at[p],
            device_id=chip_device(k), device_id_type=MESH,
        )

    def all_scattered(p):
        whole = spread.at[p]
        return pltpu.make_async_remote_copy(
            src_ref=whole, dst_ref=whole, send_sem=rs_send.at[p], recv_sem=rs_recv.at[p], device_id=twin, device_id_type=MESH
        )

    def all_shared(p):
        whole = sums.at[p, pl.ds(0, 15)]
        return pltpu.make_async_remote_copy(
            src_ref=whole, dst_ref=whole, send_sem=ag_send.at[p], recv_sem=ag_recv.at[p], device_id=twin, device_id_type=MESH
        )

    far_first = sorted(range(1, 16), key=lambda k: -min(k % 4, 4 - k % 4) - min(k // 4, 4 - k // 4))

    def each(action):
        for k in far_first:
            action(k)

    def pair_sum(p):
        exchange(p).wait_recv()
        half[p] = part[p, pl.ds(core * 16, 16)] + pair[p]

    def chip_sum(p):
        all_scattered(p).wait_recv()
        total = half[p, chip]
        for k in range(15):
            total = total + spread[p, k]
        sums[p, core * 16 + chip] = total

    def join(p):
        all_shared(p).wait_recv()
        mine = sums.at[p, pl.ds(core * 16, 16)]
        to_twin(p, 1, mine, mine).start()
        all_shared(p).wait_send()

    def coefficients(p):
        def term(side):
            rows, columns = pl.ds(side * 16, 16), pl.ds(pl.multiple_of(side * 128, 128), 128)
            return product(halves(factors[p, :, columns]), halves(sums[p, rows].reshape(128, -1)))

        coef = term(core)
        theirs = sums.at[p, pl.ds((1 - core) * 16, 16)]
        to_twin(p, 1, theirs, theirs).wait()
        coef_high[...], coef_low[...] = halves(coef + term(1 - core))

    def update():
        def step(i, carry):
            rows = pl.ds(pl.multiple_of(i * TILE, TILE), TILE)
            fresh = field[rows, :] - product((plain_high[rows, :], plain_low[rows, :]), (coef_high[...], coef_low[...]))
            field[rows, :] = fresh
            high[rows, :], low[rows, :] = halves(fresh)
            return carry

        lax.fori_loop(0, blocks, step, 0, unroll=4)

    def chain(p, slot):
        finals(p)
        inner(p, 1 - core)
        exchange(p).start()
        slot(4, 5)
        inner(p, core)
        slot(5, 6)
        pair_sum(p)
        each(lambda k: scatter(p, k).start())
        exchange(p).wait_send()
        turn(p, 0, 4)
        slot(6, 7)
        turn(p, 4, 8)
        slot(7, 10)
        chip_sum(p)
        each(lambda k: share(p, k).start())
        all_scattered(p).wait_send()
        sent(p)
        slot(10, 14)

    def finish(p):
        join(p)
        coefficients(p)

    slots(0, 0, 4)
    load_own.start()
    load_factors.start()
    load_field.wait()
    lax.fori_loop(0, blocks, split, 0)
    load_factors.wait()
    for stage in range(3):
        tell(stage)
        slots(0, 4 + 2 * stage, 6 + 2 * stage)
        hear(stage)
    slots(0, 10, 14)
    load_own.wait()

    def turn_of_panel(p, carry):
        slots(p, 0, 4)

        @pl.when(p > 1)
        def _():
            finish(p - 2)
            update()

        chain(p - 1, functools.partial(slots, p))
        return carry

    lax.fori_loop(1, panels, turn_of_panel, 0)
    finish(panels - 2)
    update()

    chain(panels - 1, lambda first, last: None)
    finish(panels - 1)


def last_update(field, plain_high, plain_low, coef_high, coef_low, out_ref, held, out_sem):
    copies = []
    for i in range(held.shape[0]):
        rows = slice(i * TILE, (i + 1) * TILE)
        held[i] = field[rows, :] - product((plain_high[rows, :], plain_low[rows, :]), (coef_high[...], coef_low[...]))
        copies.append(pltpu.make_async_copy(held.at[i], out_ref.at[rows], out_sem.at[i]))
        copies[i].start()
    for copy in copies:
        copy.wait()


def body(eigvecs, reflectors, t_factors):
    rows, columns = eigvecs.shape
    panels, block = t_factors.shape[:2]
    dma, vmem = pltpu.SemaphoreType.DMA, pltpu.VMEM
    shapes = [((rows, columns), F32), ((rows, block), BF16), ((rows, block), BF16), ((block, columns), BF16), ((block, columns), BF16)]
    own = jnp.swapaxes(reflectors, 1, 2).reshape(panels, -1, PIECE, rows)
    parts = pl.pallas_call(
        kernel,
        out_shape=[vmem(*shape) for shape in shapes],
        in_specs=[pl.BlockSpec(memory_space=pltpu.HBM)] * 3,
        out_specs=[pl.BlockSpec(memory_space=vmem)] * 5,
        scratch_shapes=[
            vmem((panels, block // PIECE, PIECE, rows), F32),
            vmem((rows, columns), BF16),
            vmem((rows, columns), BF16),
            vmem((panels, block, block), F32),
            vmem((panels, 32, 8, columns), F32),
            vmem((panels, 16, 8, columns), F32),
            vmem((panels, 16, 8, columns), F32),
            vmem((panels, 15, 8, columns), F32),
            vmem((panels, 32, 8, columns), F32),
            dma((panels, 2)),
            dma((panels, 2, 11)),
            dma((panels,)),
            dma((panels,)),
            dma((panels,)),
            dma((panels,)),
            dma((panels, 2)),
            dma((panels, 2)),
            dma((3,)),
            pltpu.SemaphoreType.REGULAR((3,)),
        ],
        compiler_params=pltpu.CompilerParams(collective_id=0, has_side_effects=True, vmem_limit_bytes=48 * 2**20),
        cost_estimate=pl.CostEstimate(flops=12 * 10**9, bytes_accessed=6 * 2**20, transcendentals=0),
    )(*(pltpu.with_memory_space_constraint(a, pltpu.HBM) for a in (eigvecs, own, t_factors)))
    return pl.pallas_call(
        last_update,
        out_shape=jax.ShapeDtypeStruct((rows, columns), F32),
        in_specs=[pl.BlockSpec(memory_space=vmem)] * 5,
        out_specs=pl.BlockSpec(memory_space=pl.ANY),
        scratch_shapes=[vmem((rows // TILE, TILE, columns), F32), dma((rows // TILE,))],
        compiler_params=pltpu.CompilerParams(vmem_limit_bytes=16 * 2**20),
        cost_estimate=pl.CostEstimate(flops=2 * 10**9, bytes_accessed=4 * 2**20, transcendentals=0),
    )(*parts)


def solution(mesh):
    in_specs = (P("rows", "cols"), P(None, "rows", "cols"), P())
    return jax.shard_map(body, mesh=mesh, in_specs=in_specs, out_specs=P("rows", "cols"), check_vma=False)
```

```python
import functools

import jax
import jax.numpy as jnp
from jax import lax
from jax.experimental import pallas as pl
from jax.experimental.pallas import tpu as pltpu
from jax.sharding import PartitionSpec as P

MESH = pl.DeviceIdType.MESH
F32, BF16 = jnp.float32, jnp.bfloat16
PIECE = 8
TILE = 256


def halves(value):
    high = value.astype(BF16)
    return high, (value - high.astype(F32)).astype(BF16)


def product(left, right):
    (left_high, left_low), (right_high, right_low) = left, right
    dot = functools.partial(jnp.dot, preferred_element_type=F32)
    return dot(left_high, right_high) + (dot(left_high, right_low) + dot(left_low, right_high))


def kernel(
    field_in, refl_in, factor_in,
    field, plain_high, plain_low, coef_high, coef_low,
    panel, high, low, factors,
    part, pair, half, spread, sums,
    z_send, z_recv, rs_send, rs_recv, ag_send, ag_recv, core_send, core_recv, in_sem, ready,
):
    row, z = lax.axis_index("rows"), lax.axis_index("cols")
    core, chip = lax.rem(row, 2), row // 2
    x, y = lax.rem(chip, 4), chip // 4
    z_next = ((row, lax.rem(z + 1, 8)), (row, lax.rem(z + 7, 8)))
    twin = (chip * 2 + 1 - core, z)

    def chip_at(k):
        return lax.rem(y + k // 4, 4) * 4 + lax.rem(x + k % 4, 4)

    def chip_device(k):
        return (chip_at(k) * 2 + core, z)

    panels, blocks = panel.shape[0], field.shape[0] // TILE

    barrier = pltpu.get_barrier_semaphore()
    beside = [chip_device(k) for k in (1, 3, 4, 12)]
    for device in (*z_next, twin, *beside):
        pl.semaphore_signal(barrier, inc=1, device_id=device, device_id_type=MESH)

    def tell(stage):
        for device in beside:
            pl.semaphore_signal(ready.at[stage], inc=1, device_id=device, device_id_type=MESH)

    def hear(stage):
        pl.semaphore_wait(ready.at[stage], len(beside))

    def split(i, carry):
        rows = pl.ds(pl.multiple_of(i * TILE, TILE), TILE)
        high[rows, :], low[rows, :] = halves(field[rows, :])
        return carry


    load_field = pltpu.make_async_copy(field_in, field, in_sem.at[0])
    load_factors = pltpu.make_async_copy(factor_in, factors, in_sem.at[1])
    load_own = pltpu.make_async_copy(refl_in, panel.at[:, pl.ds(z * 4, 4)], in_sem.at[2])
    load_field.start()
    pl.semaphore_wait(barrier, 7)

    def move(p, way, owner, c, step, source=None):
        piece = c if way == 0 else 3 - c
        place = panel.at[p, lax.rem(owner, 8) * 4 + piece]
        return pltpu.make_async_remote_copy(
            src_ref=place if source is None else source.at[p, piece], dst_ref=place, send_sem=z_send.at[p, way],
            recv_sem=z_recv.at[p, way, step * 4 + c if step < 2 or (step == 2 and c < 2) else 10],
            device_id=z_next[way], device_id_type=MESH,
        )

    def hop(p, way, s, c):
        return move(p, way, z + (8 - s if way == 0 else s), c, s, refl_in if s == 0 else None)

    def landed(p, way, s, c):
        move(p, way, z + (7 - s if way == 0 else 1 + s), c, s).wait_recv()

    def many(p, way, count):
        places = panel.at[p, pl.ds(0, count)]
        return pltpu.make_async_remote_copy(
            src_ref=places, dst_ref=places, send_sem=z_send.at[p, way], recv_sem=z_recv.at[p, way, 10],
            device_id=z_next[way], device_id_type=MESH,
        )

    def slots(p, first, last):
        for i in range(first, last):
            s, c = i // 4, i % 4
            for way in (0, 1):
                if s:
                    landed(p, way, s - 1, c)
                hop(p, way, s, c).start()

    def sent(p):
        for way in (0, 1):
            many(p, way, 14).wait_send()

    def finals(p):
        for way in (0, 1):
            many(p, way, 4).wait_recv()

    def inner(p, side):
        rows = pl.ds(side * 16, 16)
        total = 0.0
        for i in range(blocks):
            span = slice(i * TILE, (i + 1) * TILE)
            total += product(halves(panel[p, rows, :, span].reshape(128, TILE)), (high[span, :], low[span, :]))
        part[p, rows] = total.reshape(16, PIECE, -1)

    def fold(p, first, last):
        factor = halves(factors[p])

        def step(i, carry):
            rows = pl.ds(pl.multiple_of(i * TILE, TILE), TILE)
            plain = halves(panel[p, :, :, rows].reshape(256, TILE).T)
            plain_high[rows, :], plain_low[rows, :] = halves(product(plain, factor))
            return carry

        lax.fori_loop(first, last, step, 0, unroll=2)

    def to_twin(p, which, source, target):
        return pltpu.make_async_remote_copy(
            src_ref=source, dst_ref=target, send_sem=core_send.at[p, which], recv_sem=core_recv.at[p, which],
            device_id=twin, device_id_type=MESH,
        )

    def exchange(p):
        return to_twin(p, 0, part.at[p, pl.ds((1 - core) * 16, 16)], pair.at[p])

    def scatter(p, k):
        return pltpu.make_async_remote_copy(
            src_ref=half.at[p, chip_at(k)], dst_ref=spread.at[p, k - 1], send_sem=rs_send.at[p], recv_sem=rs_recv.at[p],
            device_id=chip_device(k), device_id_type=MESH,
        )

    def share(p, k):
        mine = sums.at[p, core * 16 + chip]
        return pltpu.make_async_remote_copy(
            src_ref=mine, dst_ref=mine, send_sem=ag_send.at[p], recv_sem=ag_recv.at[p],
            device_id=chip_device(k), device_id_type=MESH,
        )

    def all_scattered(p):
        whole = spread.at[p]
        return pltpu.make_async_remote_copy(
            src_ref=whole, dst_ref=whole, send_sem=rs_send.at[p], recv_sem=rs_recv.at[p], device_id=twin, device_id_type=MESH
        )

    def all_shared(p):
        whole = sums.at[p, pl.ds(0, 15)]
        return pltpu.make_async_remote_copy(
            src_ref=whole, dst_ref=whole, send_sem=ag_send.at[p], recv_sem=ag_recv.at[p], device_id=twin, device_id_type=MESH
        )

    far_first = sorted(range(1, 16), key=lambda k: -min(k % 4, 4 - k % 4) - min(k // 4, 4 - k // 4))

    def each(action):
        for k in far_first:
            action(k)

    def pair_sum(p):
        exchange(p).wait_recv()
        half[p] = part[p, pl.ds(core * 16, 16)] + pair[p]

    def chip_sum(p):
        all_scattered(p).wait_recv()
        total = half[p, chip]
        for k in range(15):
            total = total + spread[p, k]
        sums[p, core * 16 + chip] = total

    def join(p):
        all_shared(p).wait_recv()
        mine = sums.at[p, pl.ds(core * 16, 16)]
        to_twin(p, 1, mine, mine).start()
        all_shared(p).wait_send()

    def coefficients(p):
        def take(side):
            rows = pl.ds(pl.multiple_of(side * 128, 128), 128)
            coef_high[rows, :], coef_low[rows, :] = halves(sums[p, pl.ds(side * 16, 16)].reshape(128, -1))

        take(core)
        theirs = sums.at[p, pl.ds((1 - core) * 16, 16)]
        to_twin(p, 1, theirs, theirs).wait()
        take(1 - core)

    def update():
        def step(i, carry):
            rows = pl.ds(pl.multiple_of(i * TILE, TILE), TILE)
            fresh = field[rows, :] - product((plain_high[rows, :], plain_low[rows, :]), (coef_high[...], coef_low[...]))
            field[rows, :] = fresh
            high[rows, :], low[rows, :] = halves(fresh)
            return carry

        lax.fori_loop(0, blocks, step, 0, unroll=4)

    def chain(p, slot):
        finals(p)
        inner(p, 1 - core)
        exchange(p).start()
        slot(4, 5)
        inner(p, core)
        slot(5, 6)
        pair_sum(p)
        each(lambda k: scatter(p, k).start())
        exchange(p).wait_send()
        fold(p, 0, 4)
        slot(6, 7)
        fold(p, 4, 8)
        slot(7, 10)
        chip_sum(p)
        each(lambda k: share(p, k).start())
        all_scattered(p).wait_send()
        sent(p)
        slot(10, 14)

    def finish(p):
        join(p)
        coefficients(p)

    slots(0, 0, 4)
    load_own.start()
    load_factors.start()
    load_field.wait()
    lax.fori_loop(0, blocks, split, 0)
    load_factors.wait()
    for stage in range(3):
        tell(stage)
        slots(0, 4 + 2 * stage, 6 + 2 * stage)
        hear(stage)
    slots(0, 10, 14)
    load_own.wait()

    def turn_of_panel(p, carry):
        slots(p, 0, 4)

        @pl.when(p > 1)
        def _():
            finish(p - 2)
            update()

        chain(p - 1, functools.partial(slots, p))
        return carry

    lax.fori_loop(1, panels, turn_of_panel, 0)
    finish(panels - 2)
    update()

    chain(panels - 1, lambda first, last: None)
    finish(panels - 1)


def last_update(field, plain_high, plain_low, coef_high, coef_low, out_ref, held, out_sem):
    copies = []
    for i in range(held.shape[0]):
        rows = slice(i * TILE, (i + 1) * TILE)
        held[i] = field[rows, :] - product((plain_high[rows, :], plain_low[rows, :]), (coef_high[...], coef_low[...]))
        copies.append(pltpu.make_async_copy(held.at[i], out_ref.at[rows], out_sem.at[i]))
        copies[i].start()
    for copy in copies:
        copy.wait()


def body(eigvecs, reflectors, t_factors):
    rows, columns = eigvecs.shape
    panels, block = t_factors.shape[:2]
    dma, vmem = pltpu.SemaphoreType.DMA, pltpu.VMEM
    shapes = [((rows, columns), F32), ((rows, block), BF16), ((rows, block), BF16), ((block, columns), BF16), ((block, columns), BF16)]
    own = jnp.swapaxes(reflectors, 1, 2).reshape(panels, -1, PIECE, rows)
    parts = pl.pallas_call(
        kernel,
        out_shape=[vmem(*shape) for shape in shapes],
        in_specs=[pl.BlockSpec(memory_space=pltpu.HBM)] * 3,
        out_specs=[pl.BlockSpec(memory_space=vmem)] * 5,
        scratch_shapes=[
            vmem((panels, block // PIECE, PIECE, rows), F32),
            vmem((rows, columns), BF16),
            vmem((rows, columns), BF16),
            vmem((panels, block, block), F32),
            vmem((panels, 32, 8, columns), F32),
            vmem((panels, 16, 8, columns), F32),
            vmem((panels, 16, 8, columns), F32),
            vmem((panels, 15, 8, columns), F32),
            vmem((panels, 32, 8, columns), F32),
            dma((panels, 2)),
            dma((panels, 2, 11)),
            dma((panels,)),
            dma((panels,)),
            dma((panels,)),
            dma((panels,)),
            dma((panels, 2)),
            dma((panels, 2)),
            dma((3,)),
            pltpu.SemaphoreType.REGULAR((3,)),
        ],
        compiler_params=pltpu.CompilerParams(collective_id=0, has_side_effects=True, vmem_limit_bytes=48 * 2**20),
        cost_estimate=pl.CostEstimate(flops=12 * 10**9, bytes_accessed=6 * 2**20, transcendentals=0),
    )(*(pltpu.with_memory_space_constraint(a, pltpu.HBM) for a in (eigvecs, own, t_factors)))
    return pl.pallas_call(
        last_update,
        out_shape=jax.ShapeDtypeStruct((rows, columns), F32),
        in_specs=[pl.BlockSpec(memory_space=vmem)] * 5,
        out_specs=pl.BlockSpec(memory_space=pl.ANY),
        scratch_shapes=[vmem((rows // TILE, TILE, columns), F32), dma((rows // TILE,))],
        compiler_params=pltpu.CompilerParams(vmem_limit_bytes=16 * 2**20),
        cost_estimate=pl.CostEstimate(flops=2 * 10**9, bytes_accessed=4 * 2**20, transcendentals=0),
    )(*parts)


def solution(mesh):
    in_specs = (P("rows", "cols"), P(None, "rows", "cols"), P())
    return jax.shard_map(body, mesh=mesh, in_specs=in_specs, out_specs=P("rows", "cols"), check_vma=False)
```

```python
import functools

import jax
import jax.numpy as jnp
from jax import lax
from jax.experimental import pallas as pl
from jax.experimental.pallas import tpu as pltpu
from jax.sharding import PartitionSpec as P

MESH = pl.DeviceIdType.MESH
F32, BF16 = jnp.float32, jnp.bfloat16
PIECE = 8
TILE = 256


def halves(value):
    high = value.astype(BF16)
    return high, (value - high.astype(F32)).astype(BF16)


def product(left, right):
    (left_high, left_low), (right_high, right_low) = left, right
    dot = functools.partial(jnp.dot, preferred_element_type=F32)
    return dot(left_high, right_high) + (dot(left_high, right_low) + dot(left_low, right_high))


def narrow(both, twice, single):
    dot = functools.partial(jnp.dot, preferred_element_type=F32)
    return dot(both, twice) + dot(both[:, :128], single)


def kernel(
    field_in, refl_in, factor_in,
    field, out_both, out_twice, out_single,
    panel, high, low, factors, plain_high, plain_low, coef_high, coef_low, own_both,
    part, pair, half, spread, sums,
    z_send, z_recv, rs_send, rs_recv, ag_send, ag_recv, core_send, core_recv, in_sem, ready,
):
    row, z = lax.axis_index("rows"), lax.axis_index("cols")
    core, chip = lax.rem(row, 2), row // 2
    x, y = lax.rem(chip, 4), chip // 4
    z_next = ((row, lax.rem(z + 1, 8)), (row, lax.rem(z + 7, 8)))
    twin = (chip * 2 + 1 - core, z)

    def chip_at(k):
        return lax.rem(y + k // 4, 4) * 4 + lax.rem(x + k % 4, 4)

    def chip_device(k):
        return (chip_at(k) * 2 + core, z)

    panels, blocks = panel.shape[0], field.shape[0] // TILE

    barrier = pltpu.get_barrier_semaphore()
    beside = [chip_device(k) for k in (1, 3, 4, 12)]
    for device in (*z_next, twin, *beside):
        pl.semaphore_signal(barrier, inc=1, device_id=device, device_id_type=MESH)

    def tell(stage):
        for device in beside:
            pl.semaphore_signal(ready.at[stage], inc=1, device_id=device, device_id_type=MESH)

    def hear(stage):
        pl.semaphore_wait(ready.at[stage], len(beside))

    def split(i, carry):
        rows = pl.ds(pl.multiple_of(i * TILE, TILE), TILE)
        high[rows, :], low[rows, :] = halves(field[rows, :])
        return carry


    load_field = pltpu.make_async_copy(field_in, field, in_sem.at[0])
    load_factors = pltpu.make_async_copy(factor_in, factors, in_sem.at[1])
    load_own = pltpu.make_async_copy(refl_in, panel.at[:, pl.ds(z * 4, 4)], in_sem.at[2])
    load_field.start()
    pl.semaphore_wait(barrier, 7)

    def move(p, way, owner, c, step, source=None):
        piece = c if way == 0 else 3 - c
        place = panel.at[p, lax.rem(owner, 8) * 4 + piece]
        return pltpu.make_async_remote_copy(
            src_ref=place if source is None else source.at[p, piece], dst_ref=place, send_sem=z_send.at[p, way],
            recv_sem=z_recv.at[p, way, step * 4 + c if step < 2 or (step == 2 and c < 2) else 10],
            device_id=z_next[way], device_id_type=MESH,
        )

    def hop(p, way, s, c):
        return move(p, way, z + (8 - s if way == 0 else s), c, s, refl_in if s == 0 else None)

    def landed(p, way, s, c):
        move(p, way, z + (7 - s if way == 0 else 1 + s), c, s).wait_recv()

    def many(p, way, count):
        places = panel.at[p, pl.ds(0, count)]
        return pltpu.make_async_remote_copy(
            src_ref=places, dst_ref=places, send_sem=z_send.at[p, way], recv_sem=z_recv.at[p, way, 10],
            device_id=z_next[way], device_id_type=MESH,
        )

    def slots(p, first, last):
        for i in range(first, last):
            s, c = i // 4, i % 4
            for way in (0, 1):
                if s:
                    landed(p, way, s - 1, c)
                hop(p, way, s, c).start()

    def sent(p):
        for way in (0, 1):
            many(p, way, 14).wait_send()

    def finals(p):
        for way in (0, 1):
            many(p, way, 4).wait_recv()

    def inner(p, side):
        rows = pl.ds(side * 16, 16)
        total = 0.0
        for i in range(blocks):
            span = slice(i * TILE, (i + 1) * TILE)
            total += product(halves(panel[p, rows, :, span].reshape(128, TILE)), (high[span, :], low[span, :]))
        part[p, rows] = total.reshape(16, PIECE, -1)

    def fold(p, first, last, apart):
        factor = halves(factors[p])

        def step(i, carry):
            rows = pl.ds(pl.multiple_of(i * TILE, TILE), TILE)
            plain = halves(panel[p, :, :, rows].reshape(256, TILE).T)
            plain_high[rows, :], plain_low[rows, :] = halves(product(plain, factor))
            if apart:
                for side, both in ((core, own_both), (1 - core, out_both)):
                    columns = pl.ds(pl.multiple_of(side * 128, 128), 128)
                    both[rows, :128] = plain_high[rows, columns]
                    both[rows, 128:] = plain_low[rows, columns]
            return carry

        lax.fori_loop(first, last, step, 0, unroll=2)

    def to_twin(p, which, source, target):
        return pltpu.make_async_remote_copy(
            src_ref=source, dst_ref=target, send_sem=core_send.at[p, which], recv_sem=core_recv.at[p, which],
            device_id=twin, device_id_type=MESH,
        )

    def exchange(p):
        return to_twin(p, 0, part.at[p, pl.ds((1 - core) * 16, 16)], pair.at[p])

    def scatter(p, k):
        return pltpu.make_async_remote_copy(
            src_ref=half.at[p, chip_at(k)], dst_ref=spread.at[p, k - 1], send_sem=rs_send.at[p], recv_sem=rs_recv.at[p],
            device_id=chip_device(k), device_id_type=MESH,
        )

    def share(p, k):
        mine = sums.at[p, core * 16 + chip]
        return pltpu.make_async_remote_copy(
            src_ref=mine, dst_ref=mine, send_sem=ag_send.at[p], recv_sem=ag_recv.at[p],
            device_id=chip_device(k), device_id_type=MESH,
        )

    def all_scattered(p):
        whole = spread.at[p]
        return pltpu.make_async_remote_copy(
            src_ref=whole, dst_ref=whole, send_sem=rs_send.at[p], recv_sem=rs_recv.at[p], device_id=twin, device_id_type=MESH
        )

    def all_shared(p):
        whole = sums.at[p, pl.ds(0, 15)]
        return pltpu.make_async_remote_copy(
            src_ref=whole, dst_ref=whole, send_sem=ag_send.at[p], recv_sem=ag_recv.at[p], device_id=twin, device_id_type=MESH
        )

    far_first = sorted(range(1, 16), key=lambda k: -min(k % 4, 4 - k % 4) - min(k // 4, 4 - k // 4))

    def each(action):
        for k in far_first:
            action(k)

    def pair_sum(p):
        exchange(p).wait_recv()
        half[p] = part[p, pl.ds(core * 16, 16)] + pair[p]

    def chip_sum(p):
        all_scattered(p).wait_recv()
        total = half[p, chip]
        for k in range(15):
            total = total + spread[p, k]
        sums[p, core * 16 + chip] = total

    def join(p):
        all_shared(p).wait_recv()
        mine = sums.at[p, pl.ds(core * 16, 16)]
        to_twin(p, 1, mine, mine).start()
        all_shared(p).wait_send()

    def coefficients(p):
        def take(side):
            rows = pl.ds(pl.multiple_of(side * 128, 128), 128)
            coef_high[rows, :], coef_low[rows, :] = halves(sums[p, pl.ds(side * 16, 16)].reshape(128, -1))

        take(core)
        theirs = sums.at[p, pl.ds((1 - core) * 16, 16)]
        to_twin(p, 1, theirs, theirs).wait()
        take(1 - core)

    def update():
        def step(i, carry):
            rows = pl.ds(pl.multiple_of(i * TILE, TILE), TILE)
            fresh = field[rows, :] - product((plain_high[rows, :], plain_low[rows, :]), (coef_high[...], coef_low[...]))
            field[rows, :] = fresh
            high[rows, :], low[rows, :] = halves(fresh)
            return carry

        lax.fori_loop(0, blocks, step, 0, unroll=4)

    def chain(p, slot, last=False):
        finals(p)
        inner(p, 1 - core)
        exchange(p).start()
        slot(4, 5)
        inner(p, core)
        slot(5, 6)
        pair_sum(p)
        each(lambda k: scatter(p, k).start())
        exchange(p).wait_send()
        fold(p, 0, 4, last)
        slot(6, 7)
        fold(p, 4, 8, last)
        slot(7, 10)
        chip_sum(p)
        each(lambda k: share(p, k).start())
        all_scattered(p).wait_send()
        sent(p)
        slot(10, 14)

    def finish(p):
        join(p)
        coefficients(p)

    slots(0, 0, 4)
    load_own.start()
    load_factors.start()
    load_field.wait()
    lax.fori_loop(0, blocks, split, 0)
    load_factors.wait()
    for stage in range(3):
        tell(stage)
        slots(0, 4 + 2 * stage, 6 + 2 * stage)
        hear(stage)
    slots(0, 10, 14)
    load_own.wait()

    def turn_of_panel(p, carry):
        slots(p, 0, 4)

        @pl.when(p > 1)
        def _():
            finish(p - 2)
            update()

        chain(p - 1, functools.partial(slots, p))
        return carry

    lax.fori_loop(1, panels, turn_of_panel, 0)
    finish(panels - 2)
    update()


    def coefs(side):
        coef_high, coef_low = halves(sums[panels - 1, pl.ds(side * 16, 16)].reshape(128, -1))
        return jnp.concatenate([coef_high, coef_high], 0), coef_low

    chain(panels - 1, lambda first, last: None, True)
    join(panels - 1)
    twice, single = coefs(core)
    for i in range(blocks):
        rows = slice(i * TILE, (i + 1) * TILE)
        field[rows, :] -= narrow(own_both[rows, :], twice, single)
    theirs = sums.at[panels - 1, pl.ds((1 - core) * 16, 16)]
    to_twin(panels - 1, 1, theirs, theirs).wait()
    out_twice[...], out_single[...] = coefs(1 - core)


def last_update(field, both, twice, single, out_ref, held, out_sem):
    copies = []
    for i in range(held.shape[0]):
        rows = slice(i * TILE, (i + 1) * TILE)
        held[i] = field[rows, :] - narrow(both[rows, :], twice[...], single[...])
        copies.append(pltpu.make_async_copy(held.at[i], out_ref.at[rows], out_sem.at[i]))
        copies[i].start()
    for copy in copies:
        copy.wait()


def body(eigvecs, reflectors, t_factors):
    rows, columns = eigvecs.shape
    panels, block = t_factors.shape[:2]
    dma, vmem = pltpu.SemaphoreType.DMA, pltpu.VMEM
    shapes = [((rows, columns), F32), ((rows, block), BF16), ((block, columns), BF16), ((block // 2, columns), BF16)]
    own = jnp.swapaxes(reflectors, 1, 2).reshape(panels, -1, PIECE, rows)
    parts = pl.pallas_call(
        kernel,
        out_shape=[vmem(*shape) for shape in shapes],
        in_specs=[pl.BlockSpec(memory_space=pltpu.HBM)] * 3,
        out_specs=[pl.BlockSpec(memory_space=vmem)] * 4,
        scratch_shapes=[
            vmem((panels, block // PIECE, PIECE, rows), F32),
            vmem((rows, columns), BF16),
            vmem((rows, columns), BF16),
            vmem((panels, block, block), F32),
            vmem((rows, block), BF16),
            vmem((rows, block), BF16),
            vmem((block, columns), BF16),
            vmem((block, columns), BF16),
            vmem((rows, block), BF16),
            vmem((panels, 32, 8, columns), F32),
            vmem((panels, 16, 8, columns), F32),
            vmem((panels, 16, 8, columns), F32),
            vmem((panels, 15, 8, columns), F32),
            vmem((panels, 32, 8, columns), F32),
            dma((panels, 2)),
            dma((panels, 2, 11)),
            dma((panels,)),
            dma((panels,)),
            dma((panels,)),
            dma((panels,)),
            dma((panels, 2)),
            dma((panels, 2)),
            dma((3,)),
            pltpu.SemaphoreType.REGULAR((3,)),
        ],
        compiler_params=pltpu.CompilerParams(collective_id=0, has_side_effects=True, vmem_limit_bytes=48 * 2**20),
        cost_estimate=pl.CostEstimate(flops=12 * 10**9, bytes_accessed=6 * 2**20, transcendentals=0),
    )(*(pltpu.with_memory_space_constraint(a, pltpu.HBM) for a in (eigvecs, own, t_factors)))
    return pl.pallas_call(
        last_update,
        out_shape=jax.ShapeDtypeStruct((rows, columns), F32),
        in_specs=[pl.BlockSpec(memory_space=vmem)] * 4,
        out_specs=pl.BlockSpec(memory_space=pl.ANY),
        scratch_shapes=[vmem((rows // TILE, TILE, columns), F32), dma((rows // TILE,))],
        compiler_params=pltpu.CompilerParams(vmem_limit_bytes=16 * 2**20),
        cost_estimate=pl.CostEstimate(flops=2 * 10**9, bytes_accessed=4 * 2**20, transcendentals=0),
    )(*parts)


def solution(mesh):
    in_specs = (P("rows", "cols"), P(None, "rows", "cols"), P())
    return jax.shard_map(body, mesh=mesh, in_specs=in_specs, out_specs=P("rows", "cols"), check_vma=False)
```

```python
import functools

import jax
import jax.numpy as jnp
from jax import lax
from jax.experimental import pallas as pl
from jax.experimental.pallas import tpu as pltpu
from jax.sharding import PartitionSpec as P

MESH = pl.DeviceIdType.MESH
F32, BF16 = jnp.float32, jnp.bfloat16
PIECE = 8
TILE = 256


def halves(value):
    high = value.astype(BF16)
    return high, (value - high.astype(F32)).astype(BF16)


def product(left, right):
    (left_high, left_low), (right_high, right_low) = left, right
    dot = functools.partial(jnp.dot, preferred_element_type=F32)
    return dot(left_high, right_high) + (dot(left_high, right_low) + dot(left_low, right_high))


def kernel(
    field_in, refl_in, factor_in,
    field, plain_high, plain_low, coef_high, coef_low,
    panel, high, low, factors,
    part, pair, half, spread, sums,
    z_send, z_recv, rs_send, rs_recv, ag_send, ag_recv, core_send, core_recv, in_sem, ready,
):
    row, z = lax.axis_index("rows"), lax.axis_index("cols")
    core, chip = lax.rem(row, 2), row // 2
    x, y = lax.rem(chip, 4), chip // 4
    z_next = ((row, lax.rem(z + 1, 8)), (row, lax.rem(z + 7, 8)))
    twin = (chip * 2 + 1 - core, z)

    def chip_at(k):
        return lax.rem(y + k // 4, 4) * 4 + lax.rem(x + k % 4, 4)

    def chip_device(k):
        return (chip_at(k) * 2 + core, z)

    panels, blocks = panel.shape[0], field.shape[0] // TILE

    barrier = pltpu.get_barrier_semaphore()
    beside = [chip_device(k) for k in (1, 3, 4, 12)]
    for device in (*z_next, twin, *beside):
        pl.semaphore_signal(barrier, inc=1, device_id=device, device_id_type=MESH)

    def tell(stage):
        for device in beside:
            pl.semaphore_signal(ready.at[stage], inc=1, device_id=device, device_id_type=MESH)

    def hear(stage):
        pl.semaphore_wait(ready.at[stage], len(beside))

    def split(i, carry):
        rows = pl.ds(pl.multiple_of(i * TILE, TILE), TILE)
        high[rows, :], low[rows, :] = halves(field[rows, :])
        return carry


    load_field = pltpu.make_async_copy(field_in, field, in_sem.at[0])
    load_factors = pltpu.make_async_copy(factor_in, factors, in_sem.at[1])
    load_own = pltpu.make_async_copy(refl_in, panel.at[:, pl.ds(z * 4, 4)], in_sem.at[2])
    load_field.start()
    pl.semaphore_wait(barrier, 7)

    def move(p, way, owner, c, step, source=None):
        piece = c if way == 0 else 3 - c
        place = panel.at[p, lax.rem(owner, 8) * 4 + piece]
        return pltpu.make_async_remote_copy(
            src_ref=place if source is None else source.at[p, piece], dst_ref=place, send_sem=z_send.at[p, way],
            recv_sem=z_recv.at[p, way, step * 4 + c if step < 2 or (step == 2 and c < 2) else 10],
            device_id=z_next[way], device_id_type=MESH,
        )

    def hop(p, way, s, c):
        return move(p, way, z + (8 - s if way == 0 else s), c, s, refl_in if s == 0 else None)

    def landed(p, way, s, c):
        move(p, way, z + (7 - s if way == 0 else 1 + s), c, s).wait_recv()

    def many(p, way, count):
        places = panel.at[p, pl.ds(0, count)]
        return pltpu.make_async_remote_copy(
            src_ref=places, dst_ref=places, send_sem=z_send.at[p, way], recv_sem=z_recv.at[p, way, 10],
            device_id=z_next[way], device_id_type=MESH,
        )

    def slots(p, first, last):
        for i in range(first, last):
            s, c = i // 4, i % 4
            for way in (0, 1):
                if s:
                    landed(p, way, s - 1, c)
                hop(p, way, s, c).start()

    def sent(p):
        for way in (0, 1):
            many(p, way, 14).wait_send()

    def finals(p):
        for way in (0, 1):
            many(p, way, 4).wait_recv()

    def inner(p, side):
        rows = pl.ds(side * 16, 16)
        total = 0.0
        for i in range(blocks):
            span = slice(i * TILE, (i + 1) * TILE)
            total += product(halves(panel[p, rows, :, span].reshape(128, TILE)), (high[span, :], low[span, :]))
        part[p, rows] = total.reshape(16, PIECE, -1)

    def fold(p, first, last):
        factor = halves(factors[p])

        def step(i, carry):
            rows = pl.ds(pl.multiple_of(i * TILE, TILE), TILE)
            plain = halves(panel[p, :, :, rows].reshape(256, TILE).T)
            plain_high[rows, :], plain_low[rows, :] = halves(product(plain, factor))
            return carry

        lax.fori_loop(first, last, step, 0, unroll=2)

    def to_twin(p, which, source, target):
        return pltpu.make_async_remote_copy(
            src_ref=source, dst_ref=target, send_sem=core_send.at[p, which], recv_sem=core_recv.at[p, which],
            device_id=twin, device_id_type=MESH,
        )

    def exchange(p):
        return to_twin(p, 0, part.at[p, pl.ds((1 - core) * 16, 16)], pair.at[p])

    def scatter(p, k):
        return pltpu.make_async_remote_copy(
            src_ref=half.at[p, chip_at(k)], dst_ref=spread.at[p, k - 1], send_sem=rs_send.at[p], recv_sem=rs_recv.at[p],
            device_id=chip_device(k), device_id_type=MESH,
        )

    def share(p, k):
        mine = sums.at[p, core * 16 + chip]
        return pltpu.make_async_remote_copy(
            src_ref=mine, dst_ref=mine, send_sem=ag_send.at[p], recv_sem=ag_recv.at[p],
            device_id=chip_device(k), device_id_type=MESH,
        )

    def all_scattered(p):
        whole = spread.at[p]
        return pltpu.make_async_remote_copy(
            src_ref=whole, dst_ref=whole, send_sem=rs_send.at[p], recv_sem=rs_recv.at[p], device_id=twin, device_id_type=MESH
        )

    def all_shared(p):
        whole = sums.at[p, pl.ds(0, 15)]
        return pltpu.make_async_remote_copy(
            src_ref=whole, dst_ref=whole, send_sem=ag_send.at[p], recv_sem=ag_recv.at[p], device_id=twin, device_id_type=MESH
        )

    far_first = sorted(range(1, 16), key=lambda k: -min(k % 4, 4 - k % 4) - min(k // 4, 4 - k // 4))

    def each(action):
        for k in far_first:
            action(k)

    def pair_sum(p):
        exchange(p).wait_recv()
        half[p] = part[p, pl.ds(core * 16, 16)] + pair[p]

    def chip_sum(p):
        all_scattered(p).wait_recv()
        total = half[p, chip]
        for k in range(15):
            total = total + spread[p, k]
        sums[p, core * 16 + chip] = total

    def join(p):
        all_shared(p).wait_recv()
        mine = sums.at[p, pl.ds(core * 16, 16)]
        to_twin(p, 1, mine, mine).start()
        all_shared(p).wait_send()

    def coefficients(p):
        def take(side):
            rows = pl.ds(pl.multiple_of(side * 128, 128), 128)
            coef_high[rows, :], coef_low[rows, :] = halves(sums[p, pl.ds(side * 16, 16)].reshape(128, -1))

        take(core)
        theirs = sums.at[p, pl.ds((1 - core) * 16, 16)]
        to_twin(p, 1, theirs, theirs).wait()
        take(1 - core)

    def update():
        def step(i, carry):
            rows = pl.ds(pl.multiple_of(i * TILE, TILE), TILE)
            fresh = field[rows, :] - product((plain_high[rows, :], plain_low[rows, :]), (coef_high[...], coef_low[...]))
            field[rows, :] = fresh
            high[rows, :], low[rows, :] = halves(fresh)
            return carry

        lax.fori_loop(0, blocks, step, 0, unroll=8)

    def chain(p, slot):
        finals(p)
        inner(p, 1 - core)
        exchange(p).start()
        slot(4, 5)
        inner(p, core)
        slot(5, 6)
        pair_sum(p)
        each(lambda k: scatter(p, k).start())
        exchange(p).wait_send()
        fold(p, 0, 4)
        slot(6, 7)
        fold(p, 4, 8)
        slot(7, 10)
        chip_sum(p)
        each(lambda k: share(p, k).start())
        all_scattered(p).wait_send()
        sent(p)
        slot(10, 14)

    def finish(p):
        join(p)
        coefficients(p)

    slots(0, 0, 4)
    load_own.start()
    load_factors.start()
    load_field.wait()
    lax.fori_loop(0, blocks, split, 0)
    load_factors.wait()
    for stage in range(3):
        tell(stage)
        slots(0, 4 + 2 * stage, 6 + 2 * stage)
        hear(stage)
    slots(0, 10, 14)
    load_own.wait()

    def turn_of_panel(p, carry):
        slots(p, 0, 4)

        @pl.when(p > 1)
        def _():
            finish(p - 2)
            update()

        chain(p - 1, functools.partial(slots, p))
        return carry

    lax.fori_loop(1, panels, turn_of_panel, 0)
    finish(panels - 2)
    update()

    chain(panels - 1, lambda first, last: None)
    finish(panels - 1)


def last_update(field, plain_high, plain_low, coef_high, coef_low, out_ref, held, out_sem):
    copies = []
    for i in range(held.shape[0]):
        rows = slice(i * TILE, (i + 1) * TILE)
        held[i] = field[rows, :] - product((plain_high[rows, :], plain_low[rows, :]), (coef_high[...], coef_low[...]))
        copies.append(pltpu.make_async_copy(held.at[i], out_ref.at[rows], out_sem.at[i]))
        copies[i].start()
    for copy in copies:
        copy.wait()


def body(eigvecs, reflectors, t_factors):
    rows, columns = eigvecs.shape
    panels, block = t_factors.shape[:2]
    dma, vmem = pltpu.SemaphoreType.DMA, pltpu.VMEM
    shapes = [((rows, columns), F32), ((rows, block), BF16), ((rows, block), BF16), ((block, columns), BF16), ((block, columns), BF16)]
    own = jnp.swapaxes(reflectors, 1, 2).reshape(panels, -1, PIECE, rows)
    parts = pl.pallas_call(
        kernel,
        out_shape=[vmem(*shape) for shape in shapes],
        in_specs=[pl.BlockSpec(memory_space=pltpu.HBM)] * 3,
        out_specs=[pl.BlockSpec(memory_space=vmem)] * 5,
        scratch_shapes=[
            vmem((panels, block // PIECE, PIECE, rows), F32),
            vmem((rows, columns), BF16),
            vmem((rows, columns), BF16),
            vmem((panels, block, block), F32),
            vmem((panels, 32, 8, columns), F32),
            vmem((panels, 16, 8, columns), F32),
            vmem((panels, 16, 8, columns), F32),
            vmem((panels, 15, 8, columns), F32),
            vmem((panels, 32, 8, columns), F32),
            dma((panels, 2)),
            dma((panels, 2, 11)),
            dma((panels,)),
            dma((panels,)),
            dma((panels,)),
            dma((panels,)),
            dma((panels, 2)),
            dma((panels, 2)),
            dma((3,)),
            pltpu.SemaphoreType.REGULAR((3,)),
        ],
        compiler_params=pltpu.CompilerParams(collective_id=0, has_side_effects=True, vmem_limit_bytes=48 * 2**20),
        cost_estimate=pl.CostEstimate(flops=12 * 10**9, bytes_accessed=6 * 2**20, transcendentals=0),
    )(*(pltpu.with_memory_space_constraint(a, pltpu.HBM) for a in (eigvecs, own, t_factors)))
    return pl.pallas_call(
        last_update,
        out_shape=jax.ShapeDtypeStruct((rows, columns), F32),
        in_specs=[pl.BlockSpec(memory_space=vmem)] * 5,
        out_specs=pl.BlockSpec(memory_space=pl.ANY),
        scratch_shapes=[vmem((rows // TILE, TILE, columns), F32), dma((rows // TILE,))],
        compiler_params=pltpu.CompilerParams(vmem_limit_bytes=16 * 2**20),
        cost_estimate=pl.CostEstimate(flops=2 * 10**9, bytes_accessed=4 * 2**20, transcendentals=0),
    )(*parts)


def solution(mesh):
    in_specs = (P("rows", "cols"), P(None, "rows", "cols"), P())
    return jax.shard_map(body, mesh=mesh, in_specs=in_specs, out_specs=P("rows", "cols"), check_vma=False)
```
